128 devices in a mesh: seq: 16 (over z, x_lo, core), head: 8 (over x_hi, y).
Axes of the slice: x: 4 (x_hi: 2, x_lo: 2; x = x_hi * 2 + x_lo), y: 4, z: 4, core: 2. Of those that a mesh axis runs over, the one named last changes fastest.
Arguments:
- queries: bfloat16 [8192, 8192], P(('seq', 'head')), may hold values from -120 to 120
- keys: bfloat16 [8192, 1024], P(('seq', 'head')), may hold values from -5 to 5
- values: bfloat16 [8192, 1024], P(('seq', 'head')), may hold values from -5 to 5
- out_grad: bfloat16 [8192, 8192], P(('seq', 'head')), may hold values from -5 to 5
- prefix_keys: bfloat16 [256, 1024], P(None, 'head'), may hold values from -4 to 4
- prefix_values: bfloat16 [256, 1024], P(None, 'head'), may hold values from -5 to 5
- seg_ids: int32 [8192], replicated, may hold values from 0 to 31, never falling along the last dimension, each value on 1 to 1024 neighbouring positions
- prefix_lens: int32 [32], replicated, may hold values from 64 to 256, as said below
Outputs:
- query_grad: bfloat16 [8192, 8192], P(('seq', 'head'))
- key_grad: bfloat16 [8192, 1024], P(('seq', 'head'))
- value_grad: bfloat16 [8192, 1024], P(('seq', 'head'))
- prefix_key_grad: bfloat16 [256, 1024], P(None, 'head')
- prefix_value_grad: bfloat16 [256, 1024], P(None, 'head')
The draws below stay inside these ranges and needn't reach their ends.
Inputs may be any that keep to these rules, and one draw needn't show every extreme that they name: `prefix_lens`: each document sees at least the first 64 prefix tokens; some document sees all 256. `seg_ids`: each document holds at most 1024 tokens; some document holds exactly 1024.
All inputs are finite; a program needn't handle non-finite values.
Results may differ from the reference program's by a relative error of at most 0.0065.
Values may be sent and summed in bfloat16 or wider, within the bound.
A program may use at most 128 MiB of HBM per device.

```python
import math
import jax
import jax.numpy as jnp
import numpy as np
from jax import lax

HEADS = 64
KV_HEADS = 8
HEAD_DIM = 128
TOKENS = 8192
PREFIX = 256
SEGS = 32
DOC_MOST = 1024


def draw_prefix_keys(key, part):
    key = jax.random.fold_in(key, 3)
    drawn = jnp.clip(jax.random.normal(key, (PREFIX, KV_HEADS * HEAD_DIM), jnp.float32), -4.0, 4.0)
    return drawn.astype(jnp.bfloat16)


def draw_queries(key, part):
    key = jax.random.fold_in(key, 5)
    drawn = jnp.clip(jax.random.normal(key, (TOKENS, HEADS * HEAD_DIM), jnp.float32), -4.0, 4.0)
    return drawn.astype(jnp.bfloat16)


def draw_prefix_lens(key, part):
    key = jax.random.fold_in(key, 11)
    lengths = jax.random.randint(key, (SEGS,), PREFIX // 4, PREFIX + 1)
    chosen = jax.random.randint(jax.random.fold_in(key, 13), (), 0, SEGS)
    return jnp.where(jnp.arange(SEGS) == chosen, PREFIX, lengths).astype(jnp.int32)


def block_levels(own_key, shape, shards, least, largest):
    def one(position, parts):
        steps = jax.random.uniform(jax.random.fold_in(jax.random.fold_in(own_key, 6), position), (parts,), jnp.float32, least / len(shards), largest / len(shards))
        return jnp.repeat(jnp.exp(steps), shape[position] // parts).reshape((-1,) + (1,) * (len(shape) - position - 1))

    level = one(*shards[0])
    for cut in shards[1:]:
        level = level * one(*cut)
    return level


def split_up(number_of, total, limit, skew):
    weights = [(1 << 20) // math.isqrt(grade ** skew) + 1 for grade in range(2, number_of + 1)]
    rest, given = total - limit - (number_of - 1), [1] * (number_of - 1)
    while rest > 0:
        movable = [i for i in range(number_of - 1) if given[i] < limit]
        whole, budget = sum([weights[i] for i in movable]), rest
        for i in movable:
            extra = min(limit - given[i], max(1, budget * weights[i] // whole), rest)
            given[i] = given[i] + extra
            rest = rest - extra
    return np.array([limit] + given)


def uneven_parts(stream_key, number_of, total, reach, skew):
    if number_of == 2:
        one = jax.random.randint(stream_key, (), max(1, total - reach), min(reach, total - 1) + 1)
        return jnp.stack([one, total - one])
    sizes = jnp.asarray(split_up(number_of, total, reach, skew), jnp.int32)
    twos = (number_of - 1) // 2
    source_of, receiver = sizes[1:1 + 2 * twos:2], sizes[2:2 + 2 * twos:2]
    slack = jnp.minimum(source_of - 1, reach - receiver)
    shifted = jax.random.randint(jax.random.fold_in(stream_key, 1), (twos,), 0, 1 << 20) % (slack + 1)
    sizes = sizes.at[1:1 + 2 * twos:2].set(source_of - shifted).at[2:2 + 2 * twos:2].set(receiver + shifted)
    return sizes[jax.random.permutation(jax.random.fold_in(stream_key, 2), number_of)]


def normal_values(stream_key, extent, spread, most, split=(), held_as=jnp.bfloat16):
    gain = block_levels(stream_key, extent, split, -0.22, 0.18) if split else 1.0
    drawn = jax.random.normal(stream_key, extent, jnp.float32) * spread * gain
    return jnp.minimum(jnp.maximum(drawn, -most), most).astype(held_as)


def setup_inputs(seed: int = 0) -> dict:
    key_list = jax.random.split(jax.random.key(seed), 9)
    queries = draw_queries(jax.random.fold_in(key_list[8], 71), 0)
    keys = normal_values(key_list[1], (TOKENS, KV_HEADS * HEAD_DIM), 1.0, 5.0, ((0, 128),))
    values = normal_values(key_list[2], (TOKENS, KV_HEADS * HEAD_DIM), 1.0, 5.0, ((0, 128),))
    out_grad = normal_values(key_list[3], (TOKENS, HEADS * HEAD_DIM), 1.0, 5.0, ((0, 128),))
    prefix_keys = draw_prefix_keys(jax.random.fold_in(key_list[8], 71), 0)
    prefix_values = normal_values(key_list[5], (PREFIX, KV_HEADS * HEAD_DIM), 1.0, 5.0, ((1, 8),))
    seg_ids = jnp.searchsorted(jnp.cumsum(uneven_parts(key_list[6], SEGS, TOKENS, DOC_MOST, 2)), jnp.arange(TOKENS), side="right").astype(jnp.int32)
    prefix_lens = draw_prefix_lens(jax.random.fold_in(key_list[8], 71), 0)
    return {"queries": queries, "keys": keys, "values": values, "out_grad": out_grad, "prefix_keys": prefix_keys, "prefix_values": prefix_values, "seg_ids": seg_ids, "prefix_lens": prefix_lens}


def reference(queries, keys, values, out_grad, prefix_keys, prefix_values, seg_ids, prefix_lens):
    score_scale = HEAD_DIM ** -0.5
    group_size = HEADS // KV_HEADS
    block_rows = min(256, TOKENS)
    window_len = min(DOC_MOST + block_rows, TOKENS)
    block_total = TOKENS // block_rows
    labels = jnp.arange(SEGS, dtype=jnp.int32)
    limits = jnp.sum(jnp.where(seg_ids[:, None] == labels[None, :], prefix_lens[None, :], 0), axis=1)
    prefix_allowed_all = jnp.arange(PREFIX, dtype=jnp.int32)[None, :] < limits[:, None]
    slab_keys = keys.reshape(TOKENS, KV_HEADS, HEAD_DIM)
    slab_values = values.reshape(TOKENS, KV_HEADS, HEAD_DIM)
    head_pkeys = prefix_keys.reshape(PREFIX, KV_HEADS, HEAD_DIM)
    head_pvalues = prefix_values.reshape(PREFIX, KV_HEADS, HEAD_DIM)
    query_heads = queries.reshape(TOKENS, HEADS, HEAD_DIM)
    grad_heads = out_grad.reshape(TOKENS, HEADS, HEAD_DIM)

    def one_head(head_index):
        group_index = head_index // group_size
        query_head = lax.dynamic_index_in_dim(query_heads, head_index, 1, keepdims=False)
        grad_head = lax.dynamic_index_in_dim(grad_heads, head_index, 1, keepdims=False)
        slab_key_head = lax.dynamic_index_in_dim(slab_keys, group_index, 1, keepdims=False)
        slab_value_head = lax.dynamic_index_in_dim(slab_values, group_index, 1, keepdims=False)
        prefix_key_head = lax.dynamic_index_in_dim(head_pkeys, group_index, 1, keepdims=False)
        prefix_value_head = lax.dynamic_index_in_dim(head_pvalues, group_index, 1, keepdims=False)

        def block_step(carry, block_index):
            key_acc, value_acc = carry
            row_first = (block_index * block_rows).astype(jnp.int32)
            window_first = jnp.maximum(row_first + block_rows - window_len, 0).astype(jnp.int32)
            query_rows = lax.dynamic_slice_in_dim(query_head, row_first, block_rows)
            grad_rows = lax.dynamic_slice_in_dim(grad_head, row_first, block_rows)
            seg_rows = lax.dynamic_slice_in_dim(seg_ids, row_first, block_rows)
            prefix_allowed = lax.dynamic_slice_in_dim(prefix_allowed_all, row_first, block_rows)
            positions = row_first + jnp.arange(block_rows, dtype=jnp.int32)
            key_positions = window_first + jnp.arange(window_len, dtype=jnp.int32)
            key_segments = lax.dynamic_slice_in_dim(seg_ids, window_first, window_len)
            slab_allowed = (seg_rows[:, None] == key_segments[None, :]) & (key_positions[None, :] <= positions[:, None])
            allowed = jnp.concatenate([prefix_allowed, slab_allowed], axis=1)
            key_head = jnp.concatenate([prefix_key_head, lax.dynamic_slice_in_dim(slab_key_head, window_first, window_len)], axis=0)
            value_head = jnp.concatenate([prefix_value_head, lax.dynamic_slice_in_dim(slab_value_head, window_first, window_len)], axis=0)
            scores = jnp.dot(query_rows, key_head.T, preferred_element_type=jnp.float32) * score_scale
            scores = jnp.where(allowed, scores, jnp.float32(-1.0e30))
            row_peak = jnp.max(scores, axis=1)
            row_totals = jnp.sum(jnp.exp(scores - row_peak[:, None]), axis=1)
            log_totals = row_peak + jnp.log(row_totals)
            probability = jnp.exp(scores - log_totals[:, None])
            value_dots = jnp.dot(grad_rows, value_head.T, preferred_element_type=jnp.float32)
            row_delta = jnp.sum(probability * value_dots, axis=1)
            score_grad = (probability * (value_dots - row_delta[:, None])).astype(jnp.bfloat16)
            rounded_probs = probability.astype(jnp.bfloat16)
            query_part = jnp.dot(score_grad, key_head, preferred_element_type=jnp.float32) * score_scale
            key_part = jnp.dot(score_grad.T, query_rows, preferred_element_type=jnp.float32) * score_scale
            value_part = jnp.dot(rounded_probs.T, grad_rows, preferred_element_type=jnp.float32)
            slab_start = (PREFIX + window_first).astype(jnp.int32)
            key_acc = key_acc.at[:PREFIX].add(key_part[:PREFIX])
            value_acc = value_acc.at[:PREFIX].add(value_part[:PREFIX])
            old_keys = lax.dynamic_slice_in_dim(key_acc, slab_start, window_len)
            old_values = lax.dynamic_slice_in_dim(value_acc, slab_start, window_len)
            key_acc = lax.dynamic_update_slice_in_dim(key_acc, old_keys + key_part[PREFIX:], slab_start, 0)
            value_acc = lax.dynamic_update_slice_in_dim(value_acc, old_values + value_part[PREFIX:], slab_start, 0)
            return (key_acc, value_acc), query_part

        start_acc = jnp.zeros((PREFIX + TOKENS, HEAD_DIM), jnp.float32)
        (key_acc, value_acc), query_blocks = lax.scan(block_step, (start_acc, start_acc), jnp.arange(block_total, dtype=jnp.int32))
        return query_blocks.reshape(TOKENS, HEAD_DIM), key_acc, value_acc

    query_parts, key_parts, value_parts = lax.map(one_head, jnp.arange(HEADS, dtype=jnp.int32))
    query_grad = query_parts.transpose(1, 0, 2).reshape(TOKENS, HEADS * HEAD_DIM).astype(jnp.bfloat16)
    key_sum = key_parts.reshape(KV_HEADS, group_size, PREFIX + TOKENS, HEAD_DIM).sum(axis=1)
    value_sum = value_parts.reshape(KV_HEADS, group_size, PREFIX + TOKENS, HEAD_DIM).sum(axis=1)
    key_sum = key_sum.transpose(1, 0, 2).reshape(PREFIX + TOKENS, KV_HEADS * HEAD_DIM)
    value_sum = value_sum.transpose(1, 0, 2).reshape(PREFIX + TOKENS, KV_HEADS * HEAD_DIM)
    key_grad = key_sum[PREFIX:].astype(jnp.bfloat16)
    value_grad = value_sum[PREFIX:].astype(jnp.bfloat16)
    prefix_key_grad = key_sum[:PREFIX].astype(jnp.bfloat16)
    prefix_value_grad = value_sum[:PREFIX].astype(jnp.bfloat16)
    return query_grad, key_grad, value_grad, prefix_key_grad, prefix_value_grad
```

```python
import math

import jax
import jax.numpy as jnp
from jax import lax
from jax.experimental import pallas as pl
from jax.experimental.pallas import tpu as pltpu
from jax.sharding import PartitionSpec as P

MESH = pl.DeviceIdType.MESH

HEAD_DIM = 128
PREFIX = 256
RING = 4
ROWS = 64
BLOCK = RING * ROWS
BACK = 4
WINDOW = (BACK + 1) * BLOCK
KEYS = PREFIX + WINDOW
OWN = PREFIX + BACK * BLOCK
SLOTS = 2
PARTS = 4
STEPS = SLOTS * PARTS
PAIR = 2 * HEAD_DIM
GROUP = 8 * HEAD_DIM
SUB = 128
NEAR = 1024 + SUB
SPAN = PREFIX + NEAR
TILE = 128
BLOCKS = 32
SEQ = 16
SEGS = 32
SCALE = HEAD_DIM**-0.5
EXP_SCALE = SCALE / math.log(2.0)
MASKED = -1e30
PIECE = PREFIX // SEQ
AHEAD = 3


def dot_nt(a, b):
    return lax.dot_general(a, b, (((1,), (1,)), ((), ())), preferred_element_type=jnp.float32)


def dot_nn(a, b):
    return lax.dot_general(a, b, (((1,), (0,)), ((), ())), preferred_element_type=jnp.float32)


def kernel(
    q,
    g,
    k,
    v,
    pk,
    pv,
    seg,
    lens,
    dq,
    dk,
    dv,
    dpk,
    dpv,
    qb,
    gb,
    kv,
    ext,
    qx,
    kt,
    acc,
    own_sum,
    s_ref,
    d_ref,
    pb_ref,
    ds_ref,
    dqb,
    part_out,
    part_in,
    own_out,
    pre_out,
    pre_in,
    pre_sum,
    kv_local,
    kv_send,
    kv_recv,
    fix_local,
    fix_send,
    fix_recv,
    win_send,
    win_recv,
    in_local,
    in_send,
    in_recv,
    dq_local,
    dq_send,
    dq_recv,
    part_send,
    part_recv,
    own_local,
    own_send,
    own_recv,
    pre_send,
    pre_recv,
    last_local,
    last_send,
    last_recv,
):
    s = lax.axis_index("seq")
    h = lax.axis_index("head")
    y = lax.rem(h, RING)
    a = h // RING
    here = 2 * s + a

    def at_y(j):
        return (s, RING * a + lax.rem(y + j, RING))

    def at_block(b):
        return (b // 2, lax.rem(b, 2) * RING + y)

    def columns(first, size):
        return pl.ds(pl.multiple_of(first, 128), size)

    def rows_of(j):
        return pl.ds(pl.multiple_of(ROWS * j, ROWS), ROWS)

    def remote(src, dst, send, recv, device):
        return pltpu.make_async_remote_copy(
            src_ref=src,
            dst_ref=dst,
            send_sem=send,
            recv_sem=recv,
            device_id=device,
            device_id_type=MESH,
        )

    barrier = pltpu.get_barrier_semaphore()
    for j in range(1, RING):
        pl.semaphore_signal(barrier, inc=1, device_id=at_y(j), device_id_type=MESH)

    def greet(d, carry):
        there = at_block(lax.rem(here + d, BLOCKS))
        pl.semaphore_signal(barrier, inc=1, device_id=there, device_id_type=MESH)
        return carry

    lax.fori_loop(1, BLOCKS, greet, 0)
    pl.semaphore_wait(barrier, RING - 1 + BLOCKS - 1)

    def kv_own(u, t):
        src = (k, v)[t].at[:, columns((RING * u + y) * HEAD_DIM, HEAD_DIM)]
        dst = kv.at[u, t, pl.ds(pl.multiple_of(OWN + ROWS * y, ROWS), ROWS)]
        return pltpu.make_async_copy(src, dst, kv_local.at[u, t])

    def kv_copy(u, t, j):
        there = lax.rem(y + j, RING)
        src = (k, v)[t].at[:, columns((RING * u + there) * HEAD_DIM, HEAD_DIM)]
        dst = kv.at[u, t, pl.ds(pl.multiple_of(OWN + ROWS * y, ROWS), ROWS)]
        return remote(src, dst, kv_send.at[u, t, j], kv_recv.at[u, t, j], at_y(j))

    def fix_own(t):
        return pltpu.make_async_copy((pk, pv)[t], kv.at[a, t, 0:PREFIX], fix_local.at[t])

    def fix_copy(t):
        device = (s, RING * (1 - a) + y)
        return remote(
            (pk, pv)[t], kv.at[a, t, 0:PREFIX], fix_send.at[t], fix_recv.at[t], device
        )

    def win_copy(u, d):
        src = kv.at[u, :, OWN:KEYS, :]
        dst = kv.at[u, :, OWN - d * BLOCK : KEYS - d * BLOCK, :]
        device = at_block(lax.rem(here + d, BLOCKS))
        return remote(src, dst, win_send.at[u, d], win_recv.at[u, d], device)

    def in_first(n, there):
        return (RING * (n // PARTS) + there) * GROUP + lax.rem(n, PARTS) * PAIR

    def in_own(n, t):
        src = (q, g)[t].at[:, columns(in_first(n, y), PAIR)]
        return pltpu.make_async_copy(src, (qb, gb)[t].at[n, rows_of(y)], in_local.at[n, t])

    def in_copy(n, t, j):
        src = (q, g)[t].at[:, columns(in_first(n, lax.rem(y + j, RING)), PAIR)]
        dst = (qb, gb)[t].at[n, rows_of(y)]
        return remote(src, dst, in_send.at[n, t, j], in_recv.at[n, t, j], at_y(j))

    def dq_own(n):
        dst = dq.at[:, columns(in_first(n, y), PAIR)]
        return pltpu.make_async_copy(dqb.at[n, rows_of(y)], dst, dq_local.at[n])

    def dq_copy(n, j):
        src = dqb.at[n, rows_of(lax.rem(y + j, RING))]
        dst = dq.at[:, columns(in_first(n, y), PAIR)]
        return remote(src, dst, dq_send.at[n, j], dq_recv.at[n, j], at_y(j))

    def part_copy(u, d):
        device = at_block(lax.rem(here + BLOCKS - d, BLOCKS))
        return remote(
            part_out.at[u, d - 1],
            part_in.at[u, d - 1],
            part_send.at[u, d],
            part_recv.at[u, d],
            device,
        )

    def own_own(u, t):
        dst = (dk, dv)[t].at[:, columns((RING * u + y) * HEAD_DIM, HEAD_DIM)]
        return pltpu.make_async_copy(own_out.at[u, t, rows_of(y)], dst, own_local.at[u, t])

    def own_copy(u, t, j):
        src = own_out.at[u, t, rows_of(lax.rem(y + j, RING))]
        dst = (dk, dv)[t].at[:, columns((RING * u + y) * HEAD_DIM, HEAD_DIM)]
        return remote(src, dst, own_send.at[u, t, j], own_recv.at[u, t, j], at_y(j))

    def piece_rows(r):
        return pl.ds(pl.multiple_of(PIECE * r, PIECE), PIECE)

    def pre_copy(u, i):
        r = lax.rem(s + i, SEQ)
        return remote(
            pre_out.at[u, :, piece_rows(r)],
            pre_in.at[here],
            pre_send.at[u, i],
            pre_recv.at[here],
            (r, RING * u + y),
        )

    def pre_wait(b):
        return remote(
            pre_out.at[0, :, 0:PIECE], pre_in.at[b], pre_send.at[0, 0], pre_recv.at[b], (s, h)
        )

    def last_own(t):
        return pltpu.make_async_copy(
            pre_sum.at[t], (dpk, dpv)[t].at[piece_rows(s)], last_local.at[t]
        )

    def last_copy(t, i):
        return remote(
            pre_sum.at[t],
            (dpk, dpv)[t].at[piece_rows(s)],
            last_send.at[t, i],
            last_recv.at[t, i],
            (lax.rem(s + i, SEQ), h),
        )

    others = range(1, RING)
    steps_back = range(1, BACK + 1)

    def send_in(n):
        for t in range(2):
            for j in (2, 1, 3):
                in_copy(n, t, j).start()
            in_own(n, t).start()

    def send_kv(u):
        for t in range(2):
            for j in (2, 1, 3):
                kv_copy(u, t, j).start()
            kv_own(u, t).start()

    def send_windows(u):
        for t in range(2):
            kv_own(u, t).wait()
            for j in others:
                kv_copy(u, t, j).wait_recv()
        for d in steps_back:
            win_copy(u, d).start()

    send_kv(0)
    for t in range(2):
        fix_copy(t).start()
        fix_own(t).start()
    send_in(0)
    send_kv(1)

    documents = lax.broadcasted_iota(jnp.int32, (128, 128), 0)
    limits = jnp.zeros((128, 128), jnp.int32)
    for e in range(SEGS):
        limits = jnp.where(documents == e, lens[e], limits)
    lanes = lax.broadcasted_iota(jnp.int32, (128, 128), 1)
    for i in range(PREFIX // 128):
        hidden = jnp.where(lanes + 128 * i < limits, 0.0, MASKED)
        ext[128 * i : 128 * (i + 1), :] = hidden.T.astype(jnp.bfloat16)
    for i in range(WINDOW // 128):
        row = 2 * here - 2 * BACK + i
        names = jnp.broadcast_to(seg[pl.ds(jnp.maximum(row, 0), 1), :], (128, 128))
        real = jnp.full((128, 128), row, jnp.int32) >= 0
        hidden = jnp.where((names == documents) & real, 0.0, MASKED)
        ext[PREFIX + 128 * i : PREFIX + 128 * (i + 1), :] = hidden.T.astype(jnp.bfloat16)
        if i >= 2 * BACK:
            picked = jnp.where(names == documents, 1.0, 0.0)
            first = 128 * (i - 2 * BACK)
            qx[first : first + 128, :] = picked.T.astype(jnp.bfloat16)

    send_windows(0)
    for n in range(1, AHEAD):
        send_in(n)

    def prepare(u):
        for d in steps_back:
            win_copy(u, d).wait_recv()
        for i in range(KEYS // 128):
            part = kv[u, 0, 128 * i : 128 * (i + 1), :].astype(jnp.float32)
            kt[:, 128 * i : 128 * (i + 1)] = part.T.astype(jnp.bfloat16)
        acc[...] = jnp.zeros_like(acc)

    def attend(n, u, i):
        first = pl.multiple_of(SUB * i, SUB)
        rows = pl.ds(first, SUB)
        near = pl.ds(pl.multiple_of(PREFIX + first, SUB), NEAR)
        q2 = jnp.concatenate([qb[n, rows, 0:HEAD_DIM], qb[n, rows, HEAD_DIM:PAIR]], axis=0)
        g2 = jnp.concatenate([gb[n, rows, 0:HEAD_DIM], gb[n, rows, HEAD_DIM:PAIR]], axis=0)
        marks = qx[rows, :]
        q_wide = jnp.concatenate([q2, jnp.concatenate([marks, marks], axis=0)], axis=1)
        s_ref[0:PREFIX, :] = dot_nt(
            jnp.concatenate([kv[u, 0, 0:PREFIX, :], ext[0:PREFIX, :]], axis=1), q_wide
        )
        s_ref[PREFIX:SPAN, :] = dot_nt(
            jnp.concatenate([kv[u, 0, near, :], ext[near, :]], axis=1), q_wide
        )
        d_ref[0:PREFIX, :] = dot_nt(kv[u, 1, 0:PREFIX, :], g2)
        d_ref[PREFIX:SPAN, :] = dot_nt(kv[u, 1, near, :], g2)
        key_at = lax.broadcasted_iota(jnp.int32, (SUB, PAIR), 0)
        row_at = lax.rem(lax.broadcasted_iota(jnp.int32, (SUB, PAIR), 1), SUB)
        s_ref[SPAN - SUB : SPAN, :] = jnp.where(
            key_at <= row_at, s_ref[SPAN - SUB : SPAN, :], MASKED
        )

        peak = jnp.full((8, PAIR), MASKED, jnp.float32)
        for f in range(0, SPAN, TILE):
            tile = s_ref[f : f + TILE, :].reshape(TILE // 8, 8, PAIR)
            peak = jnp.maximum(peak, jnp.max(tile, axis=0))
        peak = jnp.max(peak, axis=0, keepdims=True)
        total = jnp.zeros((8, PAIR), jnp.float32)
        weighted = jnp.zeros((8, PAIR), jnp.float32)
        for f in range(0, SPAN, TILE):
            weights = jnp.exp2((s_ref[f : f + TILE, :] - peak) * EXP_SCALE)
            s_ref[f : f + TILE, :] = weights
            total += jnp.sum(weights.reshape(TILE // 8, 8, PAIR), axis=0)
            dots = weights * d_ref[f : f + TILE, :]
            weighted += jnp.sum(dots.reshape(TILE // 8, 8, PAIR), axis=0)
        total = jnp.sum(total, axis=0, keepdims=True)
        weighted = jnp.sum(weighted, axis=0, keepdims=True)
        inverse = 1.0 / total
        delta = weighted * inverse
        for f in range(0, SPAN, TILE):
            probs = s_ref[f : f + TILE, :] * inverse
            pb_ref[f : f + TILE, :] = probs.astype(jnp.bfloat16)
            ds_ref[f : f + TILE, :] = (probs * (d_ref[f : f + TILE, :] - delta)).astype(
                jnp.bfloat16
            )
        acc[1, 0:PREFIX, :] += dot_nn(pb_ref[0:PREFIX, :], g2)
        acc[1, near, :] += dot_nn(pb_ref[PREFIX:SPAN, :], g2)
        acc[0, 0:PREFIX, :] += dot_nn(ds_ref[0:PREFIX, :], q2)
        acc[0, near, :] += dot_nn(ds_ref[PREFIX:SPAN, :], q2)
        grad = dot_nn(kt[:, 0:PREFIX], ds_ref[0:PREFIX, :])
        grad += dot_nn(kt[:, near], ds_ref[PREFIX:SPAN, :])
        grad = (grad * SCALE).T.astype(jnp.bfloat16)
        dqb[n, rows, 0:HEAD_DIM] = grad[0:SUB]
        dqb[n, rows, HEAD_DIM:PAIR] = grad[SUB:PAIR]

    def close(u):
        for t in range(2):
            pre_out[u, t] = acc[t, 0:PREFIX, :].astype(jnp.bfloat16)
            for d in steps_back:
                low = OWN - d * BLOCK
                part_out[u, d - 1, t] = acc[t, low : low + BLOCK, :].astype(jnp.bfloat16)
            own_sum[u, t] = acc[t, OWN:KEYS, :]
        for d in steps_back:
            part_copy(u, d).start()

        @pl.when(a == u)
        def _():
            pre_in[here] = pre_out[u, :, piece_rows(s), :]

        @pl.when(a != u)
        def _():
            pre_copy(u, 0).start()

        def spread(i, carry):
            pre_copy(u, i).start()
            return carry

        lax.fori_loop(1, SEQ, spread, 0)

    def finish(u):
        for d in steps_back:
            part_copy(u, d).wait_recv()
        for t in range(2):
            whole = own_sum[u, t]
            for d in steps_back:
                whole += part_in[u, d - 1, t].astype(jnp.float32)
            if t == 0:
                whole = whole * SCALE
            own_out[u, t] = whole.astype(jnp.bfloat16)
        for t in range(2):
            for j in (2, 1, 3):
                own_copy(u, t, j).start()
            own_own(u, t).start()

    for t in range(2):
        fix_own(t).wait()
        fix_copy(t).wait_recv()

    def step(n, carry):
        u = n // PARTS

        @pl.when(n == 1)
        def _():
            send_windows(1)

        @pl.when(n + AHEAD < STEPS)
        def _():
            send_in(n + AHEAD)

        @pl.when(lax.rem(n, PARTS) == 0)
        def _():
            prepare(u)

        for t in range(2):
            in_own(n, t).wait()
            for j in others:
                in_copy(n, t, j).wait_recv()

        def inner(i, c):
            attend(n, u, i)
            return c

        lax.fori_loop(0, BLOCK // SUB, inner, 0)
        for j in (2, 1, 3):
            dq_copy(n, j).start()
        dq_own(n).start()

        @pl.when(lax.rem(n, PARTS) == PARTS - 1)
        def _():
            close(u)

        @pl.when(n == PARTS + 1)
        def _():
            finish(0)

        return carry

    lax.fori_loop(0, STEPS, step, 0)

    def arrive(d, carry):
        pre_wait(lax.rem(here + d, BLOCKS)).wait_recv()
        return carry

    lax.fori_loop(1, BLOCKS, arrive, 0)
    for t in range(2):
        whole = jnp.sum(pre_in[:, t].astype(jnp.float32), axis=0)
        if t == 0:
            whole = whole * SCALE
        pre_sum[t] = whole.astype(jnp.bfloat16)
    for t in range(2):
        for i in range(1, SEQ):
            last_copy(t, i).start()
        last_own(t).start()
    finish(1)

    def settle(n, carry):
        for t in range(2):
            for j in others:
                in_copy(n, t, j).wait_send()
        for j in others:
            dq_copy(n, j).wait()
        dq_own(n).wait()
        return carry

    lax.fori_loop(0, STEPS, settle, 0)
    for t in range(2):
        fix_copy(t).wait_send()
        for i in range(1, SEQ):
            last_copy(t, i).wait()
        last_own(t).wait()
    for u in range(SLOTS):
        for t in range(2):
            for j in others:
                kv_copy(u, t, j).wait_send()
                own_copy(u, t, j).wait()
            own_own(u, t).wait()
        for d in steps_back:
            win_copy(u, d).wait_send()
            part_copy(u, d).wait_send()

        @pl.when(a != u)
        def _():
            pre_copy(u, 0).wait_send()

        def sent(i, carry):
            pre_copy(u, i).wait_send()
            return carry

        lax.fori_loop(1, SEQ, sent, 0)


def on_device(queries, keys, values, out_grad, prefix_keys, prefix_values, seg_ids, prefix_lens):
    bf16, f32 = jnp.bfloat16, jnp.float32
    dma = pltpu.SemaphoreType.DMA
    hbm = pl.BlockSpec(memory_space=pl.ANY)
    arrays = [
        ((STEPS, BLOCK, PAIR), bf16),
        ((STEPS, BLOCK, PAIR), bf16),
        ((SLOTS, 2, KEYS, HEAD_DIM), bf16),
        ((KEYS, 128), bf16),
        ((BLOCK, 128), bf16),
        ((HEAD_DIM, KEYS), bf16),
        ((2, KEYS, HEAD_DIM), f32),
        ((SLOTS, 2, BLOCK, HEAD_DIM), f32),
        ((SPAN, PAIR), f32),
        ((SPAN, PAIR), f32),
        ((SPAN, PAIR), bf16),
        ((SPAN, PAIR), bf16),
        ((STEPS, BLOCK, PAIR), bf16),
        ((SLOTS, BACK, 2, BLOCK, HEAD_DIM), bf16),
        ((SLOTS, BACK, 2, BLOCK, HEAD_DIM), bf16),
        ((SLOTS, 2, BLOCK, HEAD_DIM), bf16),
        ((SLOTS, 2, PREFIX, HEAD_DIM), bf16),
        ((BLOCKS, 2, PIECE, HEAD_DIM), bf16),
        ((2, PIECE, HEAD_DIM), bf16),
    ]
    semaphores = [
        (SLOTS, 2),
        (SLOTS, 2, RING),
        (SLOTS, 2, RING),
        (2,),
        (2,),
        (2,),
        (SLOTS, BACK + 1),
        (SLOTS, BACK + 1),
        (STEPS, 2),
        (STEPS, 2, RING),
        (STEPS, 2, RING),
        (STEPS,),
        (STEPS, RING),
        (STEPS, RING),
        (SLOTS, BACK + 1),
        (SLOTS, BACK + 1),
        (SLOTS, 2),
        (SLOTS, 2, RING),
        (SLOTS, 2, RING),
        (SLOTS, SEQ),
        (BLOCKS,),
        (2,),
        (2, SEQ),
        (2, SEQ),
    ]
    return pl.pallas_call(
        kernel,
        out_shape=(
            jax.ShapeDtypeStruct(queries.shape, bf16),
            jax.ShapeDtypeStruct(keys.shape, bf16),
            jax.ShapeDtypeStruct(values.shape, bf16),
            jax.ShapeDtypeStruct(prefix_keys.shape, bf16),
            jax.ShapeDtypeStruct(prefix_values.shape, bf16),
        ),
        in_specs=[hbm] * 6
        + [pl.BlockSpec(memory_space=pltpu.VMEM), pl.BlockSpec(memory_space=pltpu.SMEM)],
        out_specs=(hbm,) * 5,
        scratch_shapes=[pltpu.VMEM(shape, kind) for shape, kind in arrays]
        + [dma(shape) for shape in semaphores],
        compiler_params=pltpu.CompilerParams(
            collective_id=0, has_side_effects=True, vmem_limit_bytes=56 * 1024 * 1024
        ),
        cost_estimate=pl.CostEstimate(
            flops=4096 * SPAN * HEAD_DIM * 10,
            bytes_accessed=4 * 1024 * 1024,
            transcendentals=4096 * SPAN,
        ),
    )(
        queries,
        out_grad,
        keys,
        values,
        prefix_keys,
        prefix_values,
        seg_ids.reshape(64, 128),
        prefix_lens,
    )


def solution(mesh):
    return jax.shard_map(
        on_device,
        mesh=mesh,
        in_specs=(
            P(("seq", "head"), None),
            P(("seq", "head"), None),
            P(("seq", "head"), None),
            P(("seq", "head"), None),
            P(None, "head"),
            P(None, "head"),
            P(),
            P(),
        ),
        out_specs=(
            P(("seq", "head"), None),
            P(("seq", "head"), None),
            P(("seq", "head"), None),
            P(None, "head"),
            P(None, "head"),
        ),
        check_vma=False,
    )
```

```python
import math

import jax
import jax.numpy as jnp
from jax import lax
from jax.experimental import pallas as pl
from jax.experimental.pallas import tpu as pltpu
from jax.sharding import PartitionSpec as P

MESH = pl.DeviceIdType.MESH

HEAD_DIM = 128
PREFIX = 256
RING = 4
ROWS = 64
BLOCK = RING * ROWS
BACK = 4
WINDOW = (BACK + 1) * BLOCK
KEYS = PREFIX + WINDOW
OWN = PREFIX + BACK * BLOCK
SLOTS = 2
PARTS = 4
STEPS = SLOTS * PARTS
PAIR = 2 * HEAD_DIM
GROUP = 8 * HEAD_DIM
SUB = 128
NEAR = 1024 + SUB
SPAN = PREFIX + NEAR
TILE = 128
BLOCKS = 32
SEQ = 16
SEGS = 32
SCALE = HEAD_DIM**-0.5
EXP_SCALE = SCALE / math.log(2.0)
MASKED = -1e30
PIECE = PREFIX // SEQ
AHEAD = 3


def dot_nt(a, b):
    return lax.dot_general(a, b, (((1,), (1,)), ((), ())), preferred_element_type=jnp.float32)


def dot_nn(a, b):
    return lax.dot_general(a, b, (((1,), (0,)), ((), ())), preferred_element_type=jnp.float32)


def kernel(
    q,
    g,
    k,
    v,
    pk,
    pv,
    seg_hbm,
    lens_hbm,
    dq,
    dk,
    dv,
    dpk,
    dpv,
    xb,
    kv,
    ext,
    qx,
    kt,
    acc,
    own_sum,
    s_ref,
    d_ref,
    pb_ref,
    ds_ref,
    dqb,
    part_out,
    part_in,
    own_out,
    pre_out,
    pre_in,
    pre_sum,
    seg,
    lens,
    small_sem,
    kv_send,
    kv_recv,
    fix_local,
    fix_send,
    fix_recv,
    win_send,
    win_recv,
    in_send,
    in_recv,
    dq_send,
    dq_recv,
    part_send,
    part_recv,
    own_send,
    own_recv,
    pre_send,
    pre_recv,
    last_send,
    last_recv,
):
    s = lax.axis_index("seq")
    h = lax.axis_index("head")
    y = lax.rem(h, RING)
    a = h // RING
    here = 2 * s + a

    def at_y(j):
        return (s, RING * a + lax.rem(y + j, RING))

    def at_block(b):
        return (b // 2, lax.rem(b, 2) * RING + y)

    def columns(first, size):
        return pl.ds(pl.multiple_of(first, 128), size)

    def rows_of(j):
        return pl.ds(pl.multiple_of(ROWS * j, ROWS), ROWS)

    def remote(src, dst, send, recv, device):
        return pltpu.make_async_remote_copy(
            src_ref=src,
            dst_ref=dst,
            send_sem=send,
            recv_sem=recv,
            device_id=device,
            device_id_type=MESH,
        )

    small = [
        pltpu.make_async_copy(seg_hbm, seg, small_sem.at[0]),
        pltpu.make_async_copy(lens_hbm, lens, small_sem.at[1]),
    ]
    for copy in small:
        copy.start()

    def wait_for(ref, sem):
        pltpu.make_async_copy(ref, ref, sem).wait()

    barrier = pltpu.get_barrier_semaphore()
    for j in range(1, RING):
        pl.semaphore_signal(barrier, inc=1, device_id=at_y(j), device_id_type=MESH)

    def greet(d, carry):
        there = at_block(lax.rem(here + d, BLOCKS))
        pl.semaphore_signal(barrier, inc=1, device_id=there, device_id_type=MESH)
        return carry

    lax.fori_loop(1, BLOCKS, greet, 0)
    pl.semaphore_wait(barrier, RING - 1 + BLOCKS - 1)

    def kv_own(u, t):
        src = (k, v)[t].at[:, columns((RING * u + y) * HEAD_DIM, HEAD_DIM)]
        dst = kv.at[u, t, pl.ds(pl.multiple_of(OWN + ROWS * y, ROWS), ROWS)]
        return pltpu.make_async_copy(src, dst, kv_recv.at[u])

    def kv_copy(u, t, j):
        there = lax.rem(y + j, RING)
        src = (k, v)[t].at[:, columns((RING * u + there) * HEAD_DIM, HEAD_DIM)]
        dst = kv.at[u, t, pl.ds(pl.multiple_of(OWN + ROWS * y, ROWS), ROWS)]
        return remote(src, dst, kv_send.at[0], kv_recv.at[u], at_y(j))

    def fix_own(t):
        return pltpu.make_async_copy((pk, pv)[t], kv.at[a, t, 0:PREFIX], fix_local.at[0])

    def fix_copy(t):
        device = (s, RING * (1 - a) + y)
        return remote(
            (pk, pv)[t], kv.at[a, t, 0:PREFIX], fix_send.at[0], fix_recv.at[0], device
        )

    def win_copy(u, d):
        src = kv.at[u, :, OWN:KEYS, :]
        dst = kv.at[u, :, OWN - d * BLOCK : KEYS - d * BLOCK, :]
        device = at_block(lax.rem(here + d, BLOCKS))
        return remote(src, dst, win_send.at[u], win_recv.at[u], device)

    def in_first(n, there):
        return (RING * (n // PARTS) + there) * GROUP + lax.rem(n, PARTS) * PAIR

    def in_own(n, t):
        src = (q, g)[t].at[:, columns(in_first(n, y), PAIR)]
        return pltpu.make_async_copy(src, xb.at[n, t, rows_of(y)], in_recv.at[n])

    def in_copy(n, t, j):
        src = (q, g)[t].at[:, columns(in_first(n, lax.rem(y + j, RING)), PAIR)]
        return remote(src, xb.at[n, t, rows_of(y)], in_send.at[t], in_recv.at[n], at_y(j))

    def dq_own(n):
        dst = dq.at[:, columns(in_first(n, y), PAIR)]
        return pltpu.make_async_copy(dqb.at[n, rows_of(y)], dst, dq_recv.at[0])

    def dq_copy(n, j):
        src = dqb.at[n, rows_of(lax.rem(y + j, RING))]
        dst = dq.at[:, columns(in_first(n, y), PAIR)]
        return remote(src, dst, dq_send.at[0], dq_recv.at[0], at_y(j))

    def part_copy(u, d):
        device = at_block(lax.rem(here + BLOCKS - d, BLOCKS))
        return remote(
            part_out.at[u, d - 1],
            part_in.at[u, d - 1],
            part_send.at[u],
            part_recv.at[u],
            device,
        )

    def own_own(u, t):
        dst = (dk, dv)[t].at[:, columns((RING * u + y) * HEAD_DIM, HEAD_DIM)]
        return pltpu.make_async_copy(own_out.at[u, t, rows_of(y)], dst, own_recv.at[t])

    def own_copy(u, t, j):
        src = own_out.at[u, t, rows_of(lax.rem(y + j, RING))]
        dst = (dk, dv)[t].at[:, columns((RING * u + y) * HEAD_DIM, HEAD_DIM)]
        return remote(src, dst, own_send.at[0], own_recv.at[t], at_y(j))

    def piece_rows(r):
        return pl.ds(pl.multiple_of(PIECE * r, PIECE), PIECE)

    def pre_copy(u, i):
        r = lax.rem(s + i, SEQ)
        return remote(
            pre_out.at[u, :, piece_rows(r)],
            pre_in.at[here],
            pre_send.at[0],
            pre_recv.at[0],
            (r, RING * u + y),
        )

    def last_own(t):
        return pltpu.make_async_copy(
            pre_sum.at[t], (dpk, dpv)[t].at[piece_rows(s)], last_recv.at[t]
        )

    def last_copy(t, i):
        return remote(
            pre_sum.at[t],
            (dpk, dpv)[t].at[piece_rows(s)],
            last_send.at[0],
            last_recv.at[t],
            (lax.rem(s + i, SEQ), h),
        )

    others = range(1, RING)
    steps_back = range(1, BACK + 1)

    def send_in(n):
        for t in range(2):
            for j in (2, 1, 3):
                in_copy(n, t, j).start()
            in_own(n, t).start()

    def send_kv(u):
        for t in range(2):
            for j in (2, 1, 3):
                kv_copy(u, t, j).start()
            kv_own(u, t).start()

    def send_windows(u):
        wait_for(kv.at[u, :, OWN:KEYS, :], kv_recv.at[u])
        for d in steps_back:
            win_copy(u, d).start()

    send_kv(0)
    for t in range(2):
        fix_copy(t).start()
        fix_own(t).start()
    send_in(0)
    send_kv(1)

    for copy in small:
        copy.wait()
    documents = lax.broadcasted_iota(jnp.int32, (128, 128), 0)
    limits = jnp.zeros((128, 128), jnp.int32)
    for e in range(SEGS):
        limits = jnp.where(documents == e, lens[e], limits)
    lanes = lax.broadcasted_iota(jnp.int32, (128, 128), 1)
    for i in range(PREFIX // 128):
        hidden = jnp.where(lanes + 128 * i < limits, 0.0, MASKED)
        ext[128 * i : 128 * (i + 1), :] = hidden.T.astype(jnp.bfloat16)
    for i in range(WINDOW // 128):
        row = 2 * here - 2 * BACK + i
        names = jnp.broadcast_to(seg[pl.ds(jnp.maximum(row, 0), 1), :], (128, 128))
        real = jnp.full((128, 128), row, jnp.int32) >= 0
        hidden = jnp.where((names == documents) & real, 0.0, MASKED)
        ext[PREFIX + 128 * i : PREFIX + 128 * (i + 1), :] = hidden.T.astype(jnp.bfloat16)
        if i >= 2 * BACK:
            picked = jnp.where(names == documents, 1.0, 0.0)
            first = 128 * (i - 2 * BACK)
            qx[first : first + 128, :] = picked.T.astype(jnp.bfloat16)

    send_windows(0)
    for n in range(1, AHEAD):
        send_in(n)

    def prepare(u):
        wait_for(kv.at[u, :, PREFIX:OWN, :], win_recv.at[u])
        for i in range(KEYS // 128):
            part = kv[u, 0, 128 * i : 128 * (i + 1), :].astype(jnp.float32)
            kt[:, 128 * i : 128 * (i + 1)] = part.T.astype(jnp.bfloat16)
        acc[...] = jnp.zeros_like(acc)

    def attend(n, u, i):
        first = pl.multiple_of(SUB * i, SUB)
        rows = pl.ds(first, SUB)
        near = pl.ds(pl.multiple_of(PREFIX + first, SUB), NEAR)
        q2 = jnp.concatenate([xb[n, 0, rows, 0:HEAD_DIM], xb[n, 0, rows, HEAD_DIM:PAIR]], axis=0)
        g2 = jnp.concatenate([xb[n, 1, rows, 0:HEAD_DIM], xb[n, 1, rows, HEAD_DIM:PAIR]], axis=0)
        marks = qx[rows, :]
        q_wide = jnp.concatenate([q2, jnp.concatenate([marks, marks], axis=0)], axis=1)
        s_ref[0:PREFIX, :] = dot_nt(
            jnp.concatenate([kv[u, 0, 0:PREFIX, :], ext[0:PREFIX, :]], axis=1), q_wide
        )
        s_ref[PREFIX:SPAN, :] = dot_nt(
            jnp.concatenate([kv[u, 0, near, :], ext[near, :]], axis=1), q_wide
        )
        d_ref[0:PREFIX, :] = dot_nt(kv[u, 1, 0:PREFIX, :], g2)
        d_ref[PREFIX:SPAN, :] = dot_nt(kv[u, 1, near, :], g2)
        key_at = lax.broadcasted_iota(jnp.int32, (SUB, PAIR), 0)
        row_at = lax.rem(lax.broadcasted_iota(jnp.int32, (SUB, PAIR), 1), SUB)
        s_ref[SPAN - SUB : SPAN, :] = jnp.where(
            key_at <= row_at, s_ref[SPAN - SUB : SPAN, :], MASKED
        )

        peak = jnp.full((8, PAIR), MASKED, jnp.float32)
        for f in range(0, SPAN, TILE):
            tile = s_ref[f : f + TILE, :].reshape(TILE // 8, 8, PAIR)
            peak = jnp.maximum(peak, jnp.max(tile, axis=0))
        peak = jnp.max(peak, axis=0, keepdims=True)
        total = jnp.zeros((8, PAIR), jnp.float32)
        weighted = jnp.zeros((8, PAIR), jnp.float32)
        for f in range(0, SPAN, TILE):
            weights = jnp.exp2((s_ref[f : f + TILE, :] - peak) * EXP_SCALE)
            s_ref[f : f + TILE, :] = weights
            total += jnp.sum(weights.reshape(TILE // 8, 8, PAIR), axis=0)
            dots = weights * d_ref[f : f + TILE, :]
            weighted += jnp.sum(dots.reshape(TILE // 8, 8, PAIR), axis=0)
        total = jnp.sum(total, axis=0, keepdims=True)
        weighted = jnp.sum(weighted, axis=0, keepdims=True)
        inverse = 1.0 / total
        delta = weighted * inverse
        for f in range(0, SPAN, TILE):
            probs = s_ref[f : f + TILE, :] * inverse
            pb_ref[f : f + TILE, :] = probs.astype(jnp.bfloat16)
            ds_ref[f : f + TILE, :] = (probs * (d_ref[f : f + TILE, :] - delta)).astype(
                jnp.bfloat16
            )
        acc[1, 0:PREFIX, :] += dot_nn(pb_ref[0:PREFIX, :], g2)
        acc[1, near, :] += dot_nn(pb_ref[PREFIX:SPAN, :], g2)
        acc[0, 0:PREFIX, :] += dot_nn(ds_ref[0:PREFIX, :], q2)
        acc[0, near, :] += dot_nn(ds_ref[PREFIX:SPAN, :], q2)
        grad = dot_nn(kt[:, 0:PREFIX], ds_ref[0:PREFIX, :])
        grad += dot_nn(kt[:, near], ds_ref[PREFIX:SPAN, :])
        grad = (grad * SCALE).T.astype(jnp.bfloat16)
        dqb[n, rows, 0:HEAD_DIM] = grad[0:SUB]
        dqb[n, rows, HEAD_DIM:PAIR] = grad[SUB:PAIR]

    def close(u):
        for t in range(2):
            pre_out[u, t] = acc[t, 0:PREFIX, :].astype(jnp.bfloat16)
            for d in steps_back:
                low = OWN - d * BLOCK
                part_out[u, d - 1, t] = acc[t, low : low + BLOCK, :].astype(jnp.bfloat16)
            own_sum[u, t] = acc[t, OWN:KEYS, :]
        for d in steps_back:
            part_copy(u, d).start()

        @pl.when(a == u)
        def _():
            pre_in[here] = pre_out[u, :, piece_rows(s), :]

        @pl.when(a != u)
        def _():
            pre_copy(u, 0).start()

        def spread(i, carry):
            pre_copy(u, i).start()
            return carry

        lax.fori_loop(1, SEQ, spread, 0)

    def finish(u):
        wait_for(part_in.at[u], part_recv.at[u])
        for t in range(2):
            whole = own_sum[u, t]
            for d in steps_back:
                whole += part_in[u, d - 1, t].astype(jnp.float32)
            if t == 0:
                whole = whole * SCALE
            own_out[u, t] = whole.astype(jnp.bfloat16)
        for t in range(2):
            for j in (2, 1, 3):
                own_copy(u, t, j).start()
            own_own(u, t).start()

    wait_for(kv.at[0, :, 0:PREFIX], fix_local.at[0])
    wait_for(kv.at[0, :, 0:PREFIX], fix_recv.at[0])

    def step(n, carry):
        u = n // PARTS

        @pl.when(n == 1)
        def _():
            send_windows(1)

        @pl.when(n + AHEAD < STEPS)
        def _():
            send_in(n + AHEAD)

        @pl.when(lax.rem(n, PARTS) == 0)
        def _():
            prepare(u)

        wait_for(xb.at[n], in_recv.at[n])

        def inner(i, c):
            attend(n, u, i)
            return c

        lax.fori_loop(0, BLOCK // SUB, inner, 0)
        for j in (2, 1, 3):
            dq_copy(n, j).start()
        dq_own(n).start()

        @pl.when(lax.rem(n, PARTS) == PARTS - 1)
        def _():
            close(u)

        @pl.when(n == PARTS + 1)
        def _():
            finish(0)

        return carry

    lax.fori_loop(0, STEPS, step, 0)

    wait_for(pre_in.at[0 : BLOCKS - 1], pre_recv.at[0])
    for t in range(2):
        whole = jnp.sum(pre_in[:, t].astype(jnp.float32), axis=0)
        if t == 0:
            whole = whole * SCALE
        pre_sum[t] = whole.astype(jnp.bfloat16)
    for t in range(2):
        for i in range(1, SEQ):
            last_copy(t, i).start()
        last_own(t).start()
    finish(1)

    for t in range(2):
        wait_for(xb.at[0:6, t], in_send.at[t])
        wait_for((dk, dv)[t], own_recv.at[t])
        wait_for((dpk, dpv)[t], last_recv.at[t])
    wait_for(dqb.at[0:6], dq_send.at[0])
    wait_for(dq, dq_recv.at[0])
    wait_for(own_out.at[:, :, 0 : BLOCK - ROWS], kv_send.at[0])
    wait_for(own_out.at[:, :, 0 : BLOCK - ROWS], own_send.at[0])
    wait_for(pre_out.at[0], fix_send.at[0])
    wait_for(pre_out.at[0, :, 0 : PREFIX - PIECE], last_send.at[0])
    wait_for(pre_in.at[0 : BLOCKS - 1], pre_send.at[0])
    for u in range(SLOTS):
        wait_for(kv.at[u, :, PREFIX:OWN, :], win_send.at[u])
        wait_for(part_out.at[u], part_send.at[u])


def hand_over(*refs):
    count = (len(refs) - 2) // 3
    before, after, held = refs[:count], refs[count : 2 * count], refs[2 * count : 3 * count]
    arrived, stored = refs[-2:]
    pieces = []
    for i in range(count):
        rows = before[i].shape[0]
        size = 16 if before[i].shape[1] > GROUP else rows
        for first in range(0, rows, size):
            n = len(pieces)
            part = pl.ds(first, size)
            pieces.append(
                (
                    pltpu.make_async_copy(before[i].at[part], held[i].at[part], arrived.at[n]),
                    pltpu.make_async_copy(held[i].at[part], after[i].at[part], stored.at[n]),
                )
            )
    for load, store in pieces:
        load.start()
    for load, store in pieces:
        load.wait()
        store.start()
    for load, store in pieces:
        store.wait()


def on_device(queries, keys, values, out_grad, prefix_keys, prefix_values, seg_ids, prefix_lens):
    bf16, f32 = jnp.bfloat16, jnp.float32
    dma = pltpu.SemaphoreType.DMA
    hbm = pl.BlockSpec(memory_space=pl.ANY)
    arrays = [
        ((STEPS, 2, BLOCK, PAIR), bf16),
        ((SLOTS, 2, KEYS, HEAD_DIM), bf16),
        ((KEYS, 128), bf16),
        ((BLOCK, 128), bf16),
        ((HEAD_DIM, KEYS), bf16),
        ((2, KEYS, HEAD_DIM), f32),
        ((SLOTS, 2, BLOCK, HEAD_DIM), f32),
        ((SPAN, PAIR), f32),
        ((SPAN, PAIR), f32),
        ((SPAN, PAIR), bf16),
        ((SPAN, PAIR), bf16),
        ((STEPS, BLOCK, PAIR), bf16),
        ((SLOTS, BACK, 2, BLOCK, HEAD_DIM), bf16),
        ((SLOTS, BACK, 2, BLOCK, HEAD_DIM), bf16),
        ((SLOTS, 2, BLOCK, HEAD_DIM), bf16),
        ((SLOTS, 2, PREFIX, HEAD_DIM), bf16),
        ((BLOCKS, 2, PIECE, HEAD_DIM), bf16),
        ((2, PIECE, HEAD_DIM), bf16),
    ]
    semaphores = [
        2,
        1,
        SLOTS,
        1,
        1,
        1,
        SLOTS,
        SLOTS,
        2,
        STEPS,
        1,
        1,
        SLOTS,
        SLOTS,
        1,
        2,
        1,
        1,
        1,
        2,
    ]
    results = (
        jax.ShapeDtypeStruct(queries.shape, bf16),
        jax.ShapeDtypeStruct(keys.shape, bf16),
        jax.ShapeDtypeStruct(values.shape, bf16),
        jax.ShapeDtypeStruct(prefix_keys.shape, bf16),
        jax.ShapeDtypeStruct(prefix_values.shape, bf16),
    )
    raw = pl.pallas_call(
        kernel,
        out_shape=results,
        in_specs=[hbm] * 8,
        out_specs=(hbm,) * 5,
        scratch_shapes=[pltpu.VMEM(shape, kind) for shape, kind in arrays]
        + [pltpu.VMEM((64, 128), jnp.int32), pltpu.SMEM((SEGS,), jnp.int32)]
        + [dma((size,)) for size in semaphores],
        compiler_params=pltpu.CompilerParams(
            collective_id=0, has_side_effects=True, vmem_limit_bytes=56 * 1024 * 1024
        ),
        cost_estimate=pl.CostEstimate(
            flops=4096 * SPAN * HEAD_DIM * 10,
            bytes_accessed=4 * 1024 * 1024,
            transcendentals=4096 * SPAN,
        ),
    )(
        queries,
        out_grad,
        keys,
        values,
        prefix_keys,
        prefix_values,
        seg_ids.reshape(64, 128),
        prefix_lens,
    )
    return pl.pallas_call(
        hand_over,
        out_shape=results,
        in_specs=[hbm] * len(results),
        out_specs=(hbm,) * len(results),
        scratch_shapes=[pltpu.VMEM(x.shape, x.dtype) for x in results] + [dma((16,)), dma((16,))],
    )(*raw)


def solution(mesh):
    return jax.shard_map(
        on_device,
        mesh=mesh,
        in_specs=(
            P(("seq", "head"), None),
            P(("seq", "head"), None),
            P(("seq", "head"), None),
            P(("seq", "head"), None),
            P(None, "head"),
            P(None, "head"),
            P(),
            P(),
        ),
        out_specs=(
            P(("seq", "head"), None),
            P(("seq", "head"), None),
            P(("seq", "head"), None),
            P(None, "head"),
            P(None, "head"),
        ),
        check_vma=False,
    )
```

```python
import math

import jax
import jax.numpy as jnp
from jax import lax
from jax.experimental import pallas as pl
from jax.experimental.pallas import tpu as pltpu
from jax.sharding import PartitionSpec as P

MESH = pl.DeviceIdType.MESH

HEAD_DIM = 128
PREFIX = 256
RING = 4
ROWS = 64
BLOCK = RING * ROWS
BACK = 4
WINDOW = (BACK + 1) * BLOCK
KEYS = PREFIX + WINDOW
OWN = PREFIX + BACK * BLOCK
SLOTS = 2
HEADS = 4
PARTS = 2
STEPS = SLOTS * PARTS
WIDE = HEADS * HEAD_DIM
GROUP = PARTS * WIDE
SUB = 128
NEAR = 1024 + SUB
SPAN = PREFIX + NEAR
TILE = 128
HALF = 256
CUTS = [(0, PREFIX)] + [(PREFIX + NEAR // 3 * i, NEAR // 3) for i in range(3)]
BLOCKS = 32
SEQ = 16
SEGS = 32
SCALE = HEAD_DIM**-0.5
EXP_SCALE = SCALE / math.log(2.0)
MASKED = -1e30
PIECE = PREFIX // SEQ


def dot_nt(a, b):
    return lax.dot_general(a, b, (((1,), (1,)), ((), ())), preferred_element_type=jnp.float32)


def dot_nn(a, b):
    return lax.dot_general(a, b, (((1,), (0,)), ((), ())), preferred_element_type=jnp.float32)


def kernel(
    q,
    g,
    k,
    v,
    pk,
    pv,
    seg_hbm,
    lens_hbm,
    dq,
    dk,
    dv,
    dpk,
    dpv,
    xb,
    kv,
    ext,
    qx,
    kt,
    acc,
    own_sum,
    s_0,
    d_0,
    p_0,
    ds_0,
    s_1,
    d_1,
    p_1,
    ds_1,
    dqb,
    part_out,
    part_in,
    own_out,
    pre_out,
    pre_in,
    pre_sum,
    seg,
    lens,
    small_sem,
    kv_send,
    kv_recv,
    fix_local,
    fix_send,
    fix_recv,
    win_send,
    win_recv,
    in_send,
    in_recv,
    dq_send,
    dq_recv,
    part_send,
    part_recv,
    own_send,
    own_recv,
    pre_send,
    pre_recv,
    last_send,
    last_recv,
):
    s = lax.axis_index("seq")
    h = lax.axis_index("head")
    y = lax.rem(h, RING)
    a = h // RING
    here = 2 * s + a

    def at_y(j):
        return (s, RING * a + lax.rem(y + j, RING))

    def at_block(b):
        return (b // 2, lax.rem(b, 2) * RING + y)

    def columns(first, size):
        return pl.ds(pl.multiple_of(first, 128), size)

    def rows_of(j):
        return pl.ds(pl.multiple_of(ROWS * j, ROWS), ROWS)

    def remote(src, dst, send, recv, device):
        return pltpu.make_async_remote_copy(
            src_ref=src,
            dst_ref=dst,
            send_sem=send,
            recv_sem=recv,
            device_id=device,
            device_id_type=MESH,
        )

    small = [
        pltpu.make_async_copy(seg_hbm, seg, small_sem.at[0]),
        pltpu.make_async_copy(lens_hbm, lens, small_sem.at[1]),
    ]
    for copy in small:
        copy.start()

    def wait_for(ref, sem):
        pltpu.make_async_copy(ref, ref, sem).wait()

    barrier = pltpu.get_barrier_semaphore()
    for j in range(1, RING):
        pl.semaphore_signal(barrier, inc=1, device_id=at_y(j), device_id_type=MESH)

    def greet(d, carry):
        there = at_block(lax.rem(here + d, BLOCKS))
        pl.semaphore_signal(barrier, inc=1, device_id=there, device_id_type=MESH)
        return carry

    lax.fori_loop(1, BLOCKS, greet, 0)
    def kv_own(u, t):
        src = (k, v)[t].at[:, columns((RING * u + y) * HEAD_DIM, HEAD_DIM)]
        dst = kv.at[u, t, pl.ds(pl.multiple_of(OWN + ROWS * y, ROWS), ROWS)]
        return pltpu.make_async_copy(src, dst, kv_recv.at[u])

    def kv_copy(u, t, j):
        there = lax.rem(y + j, RING)
        src = (k, v)[t].at[:, columns((RING * u + there) * HEAD_DIM, HEAD_DIM)]
        dst = kv.at[u, t, pl.ds(pl.multiple_of(OWN + ROWS * y, ROWS), ROWS)]
        return remote(src, dst, kv_send.at[0], kv_recv.at[u], at_y(j))

    def fix_own(t):
        return pltpu.make_async_copy((pk, pv)[t], kv.at[a, t, 0:PREFIX], fix_local.at[0])

    def fix_copy(t):
        device = (s, RING * (1 - a) + y)
        return remote(
            (pk, pv)[t], kv.at[a, t, 0:PREFIX], fix_send.at[0], fix_recv.at[0], device
        )

    def win_copy(u, d):
        src = kv.at[u, :, OWN:KEYS, :]
        dst = kv.at[u, :, OWN - d * BLOCK : KEYS - d * BLOCK, :]
        device = at_block(lax.rem(here + d, BLOCKS))
        return remote(src, dst, win_send.at[u], win_recv.at[u], device)

    def in_first(n, there):
        return (RING * (n // PARTS) + there) * GROUP + lax.rem(n, PARTS) * WIDE

    def in_own(n, t):
        src = (q, g)[t].at[:, columns(in_first(n, y), WIDE)]
        return pltpu.make_async_copy(src, xb.at[n, t, rows_of(y)], in_recv.at[n])

    def in_copy(n, t, j):
        src = (q, g)[t].at[:, columns(in_first(n, lax.rem(y + j, RING)), WIDE)]
        return remote(src, xb.at[n, t, rows_of(y)], in_send.at[t], in_recv.at[n], at_y(j))

    def dq_own(n):
        dst = dq.at[:, columns(in_first(n, y), WIDE)]
        return pltpu.make_async_copy(dqb.at[n, rows_of(y)], dst, dq_recv.at[0])

    def dq_copy(n, j):
        src = dqb.at[n, rows_of(lax.rem(y + j, RING))]
        dst = dq.at[:, columns(in_first(n, y), WIDE)]
        return remote(src, dst, dq_send.at[0], dq_recv.at[0], at_y(j))

    def part_copy(u, t, d):
        device = at_block(lax.rem(here + BLOCKS - d, BLOCKS))
        return remote(
            part_out.at[u, t, d - 1],
            part_in.at[u, t, d - 1],
            part_send.at[u, t],
            part_recv.at[u, t],
            device,
        )

    def own_own(u, t):
        dst = (dk, dv)[t].at[:, columns((RING * u + y) * HEAD_DIM, HEAD_DIM)]
        return pltpu.make_async_copy(own_out.at[u, t, rows_of(y)], dst, own_recv.at[t])

    def own_copy(u, t, j):
        src = own_out.at[u, t, rows_of(lax.rem(y + j, RING))]
        dst = (dk, dv)[t].at[:, columns((RING * u + y) * HEAD_DIM, HEAD_DIM)]
        return remote(src, dst, own_send.at[0], own_recv.at[t], at_y(j))

    def piece_rows(r):
        return pl.ds(pl.multiple_of(PIECE * r, PIECE), PIECE)

    def pre_copy(u, i):
        r = lax.rem(s + i, SEQ)
        return remote(
            pre_out.at[u, :, piece_rows(r)],
            pre_in.at[here],
            pre_send.at[0],
            pre_recv.at[0],
            (r, RING * u + y),
        )

    def last_own(t):
        return pltpu.make_async_copy(
            pre_sum.at[t], (dpk, dpv)[t].at[piece_rows(s)], last_recv.at[t]
        )

    def last_copy(t, i):
        return remote(
            pre_sum.at[t],
            (dpk, dpv)[t].at[piece_rows(s)],
            last_send.at[0],
            last_recv.at[t],
            (lax.rem(s + i, SEQ), h),
        )

    others = range(1, RING)
    steps_back = range(1, BACK + 1)

    def send_in(n):
        for t in range(2):
            for j in (2, 1, 3):
                in_copy(n, t, j).start()

    def send_kv(u):
        for t in range(2):
            for j in (2, 1, 3):
                kv_copy(u, t, j).start()

    def send_windows(u):
        wait_for(kv.at[u, :, OWN:KEYS, :], kv_recv.at[u])
        for d in steps_back:
            win_copy(u, d).start()

    for t in range(2):
        for u in range(SLOTS):
            kv_own(u, t).start()
        fix_own(t).start()
    for n in range(STEPS):
        for t in range(2):
            in_own(n, t).start()

    for copy in small:
        copy.wait()
    documents = lax.broadcasted_iota(jnp.int32, (128, 128), 0)
    limits = jnp.zeros((128, 128), jnp.int32)
    for e in range(SEGS):
        limits = jnp.where(documents == e, lens[e], limits)
    lanes = lax.broadcasted_iota(jnp.int32, (128, 128), 1)
    for i in range(PREFIX // 128):
        hidden = jnp.where(lanes + 128 * i < limits, 0.0, MASKED)
        ext[128 * i : 128 * (i + 1), :] = hidden.T.astype(jnp.bfloat16)
    for i in range(WINDOW // 128):
        row = 2 * here - 2 * BACK + i
        names = jnp.broadcast_to(seg[pl.ds(jnp.maximum(row, 0), 1), :], (128, 128))
        real = jnp.full((128, 128), row, jnp.int32) >= 0
        hidden = jnp.where((names == documents) & real, 0.0, MASKED)
        ext[PREFIX + 128 * i : PREFIX + 128 * (i + 1), :] = hidden.T.astype(jnp.bfloat16)
        if i >= 2 * BACK:
            picked = jnp.where(names == documents, 1.0, 0.0)
            first = 128 * (i - 2 * BACK)
            qx[first : first + 128, :] = picked.T.astype(jnp.bfloat16)

    pl.semaphore_wait(barrier, RING - 1 + BLOCKS - 1)
    send_kv(0)
    for t in range(2):
        fix_copy(t).start()
    send_in(0)
    send_kv(1)

    send_windows(0)
    for n in range(1, STEPS):
        send_in(n)

    def prepare(u):
        wait_for(kv.at[u, :, PREFIX:OWN, :], win_recv.at[u])
        for i in range(KEYS // 128):
            part = kv[u, 0, 128 * i : 128 * (i + 1), :].astype(jnp.float32)
            kt[:, 128 * i : 128 * (i + 1)] = part.T.astype(jnp.bfloat16)
        acc[...] = jnp.zeros_like(acc)

    passes = ((s_0, d_0, p_0, ds_0), (s_1, d_1, p_1, ds_1))

    def key_rows(i, cut):
        first, size = cut
        return pl.ds(first if first < PREFIX else first + SUB * i, size)

    def load_rows(n, t, i):
        rows = pl.ds(SUB * i, SUB)
        return jnp.concatenate(
            [xb[n, t, rows, HEAD_DIM * x : HEAD_DIM * (x + 1)] for x in range(HEADS)], axis=0
        )

    def score(u, i, q2, g2):
        s_ref, d_ref, _, _ = passes[i]
        marks = jnp.concatenate([qx[pl.ds(SUB * i, SUB), :]] * HEADS, axis=0)
        q_wide = jnp.concatenate([q2, marks], axis=1)

        def keys(cut):
            rows = key_rows(i, cut)
            wide = jnp.concatenate([kv[u, 0, rows, :], ext[rows, :]], axis=1)
            s_ref[pl.ds(*cut), :] = dot_nt(wide, q_wide)

        def values(cut):
            d_ref[pl.ds(*cut), :] = dot_nt(kv[u, 1, key_rows(i, cut), :], g2)

        for cut in CUTS:
            yield lambda: keys(cut)
        for cut in CUTS:
            yield lambda: values(cut)

    def weigh(i, first):
        s_ref, d_ref, p_ref, ds_ref = passes[i]
        tiles = [pl.ds(f, TILE) for f in range(0, SPAN, TILE)]
        key_at = lax.broadcasted_iota(jnp.int32, (SUB, HALF), 0)
        row_at = lax.rem(lax.broadcasted_iota(jnp.int32, (SUB, HALF), 1), SUB)

        def fold(tile):
            return tile.reshape(TILE // 8, 8, HALF)

        for c in range(0, WIDE, HALF):
            cols = pl.ds(c, HALF)
            out = pl.ds(pl.multiple_of(first + c, HALF), HALF)
            has = {}

            def begin():
                last = pl.ds(SPAN - SUB, SUB)
                s_ref[last, cols] = jnp.where(key_at <= row_at, s_ref[last, cols], MASKED)
                has["peak"] = jnp.full((8, HALF), MASKED, jnp.float32)
                has["total"] = jnp.zeros((8, HALF), jnp.float32)
                has["weighted"] = jnp.zeros((8, HALF), jnp.float32)

            def top(tile):
                has["peak"] = jnp.maximum(has["peak"], jnp.max(fold(s_ref[tile, cols]), axis=0))

            def level():
                has["peak"] = jnp.max(has["peak"], axis=0, keepdims=True)

            def weight(tile):
                weights = jnp.exp2((s_ref[tile, cols] - has["peak"]) * EXP_SCALE)
                s_ref[tile, cols] = weights
                has["total"] += jnp.sum(fold(weights), axis=0)
                has["weighted"] += jnp.sum(fold(weights * d_ref[tile, cols]), axis=0)

            def settle():
                has["inverse"] = 1.0 / jnp.sum(has["total"], axis=0, keepdims=True)
                weighted = jnp.sum(has["weighted"], axis=0, keepdims=True)
                has["delta"] = weighted * has["inverse"]

            def grade(tile):
                probs = s_ref[tile, cols] * has["inverse"]
                p_ref[tile, cols] = probs.astype(jnp.bfloat16)
                score_grad = probs * (d_ref[tile, cols] - has["delta"])
                ds_ref[tile, out] = score_grad.astype(jnp.bfloat16)

            yield begin
            for tile in tiles:
                yield lambda: top(tile)
            yield level
            for tile in tiles:
                yield lambda: weight(tile)
            yield settle
            for tile in tiles:
                yield lambda: grade(tile)

    def gather_up(i, first, q2, g2):
        _, _, p_ref, ds_ref = passes[i]
        cols = pl.ds(pl.multiple_of(first, WIDE), WIDE)

        def values(cut):
            acc[1, key_rows(i, cut), :] += dot_nn(p_ref[pl.ds(*cut), :], g2)

        def keys(cut):
            acc[0, key_rows(i, cut), :] += dot_nn(ds_ref[pl.ds(*cut), cols], q2)

        for cut in CUTS:
            yield lambda: values(cut)
        for cut in CUTS:
            yield lambda: keys(cut)

    def together(products, count, others, other_count):
        done = 0
        for i in range(other_count):
            while done < count and done * other_count <= i * count:
                next(products)()
                done += 1
            next(others)()
        for rest in products:
            rest()

    def attend(n, u):
        first = lax.rem(n, PARTS) * WIDE
        held = [[load_rows(n, t, i) for t in range(2)] for i in range(2)]
        products = 2 * len(CUTS)
        passing = WIDE // HALF * (3 * (SPAN // TILE) + 3)
        for do in score(u, 0, *held[0]):
            do()
        together(score(u, 1, *held[1]), products, weigh(0, first), passing)
        together(gather_up(0, first, *held[0]), products, weigh(1, first), passing)
        for do in gather_up(1, first, *held[1]):
            do()

    def query_part(u):
        for i in range(2):
            _, _, _, ds_ref = passes[i]
            rows = pl.ds(SUB * i, SUB)
            near = pl.ds(PREFIX + SUB * i, NEAR)
            grad = dot_nn(kt[:, 0:PREFIX], ds_ref[0:PREFIX, :])
            grad += dot_nn(kt[:, near], ds_ref[PREFIX:SPAN, :])
            grad = (grad * SCALE).T.astype(jnp.bfloat16)
            for x in range(PARTS * HEADS):
                cols = pl.ds(HEAD_DIM * (x % HEADS), HEAD_DIM)
                dqb[PARTS * u + x // HEADS, rows, cols] = grad[SUB * x : SUB * (x + 1)]
        for n in range(PARTS):
            for j in (2, 1, 3):
                dq_copy(PARTS * u + n, j).start()
            dq_own(PARTS * u + n).start()

    def close(u):
        for t in (1, 0):
            for d in steps_back:
                low = OWN - d * BLOCK
                part_out[u, t, d - 1] = acc[t, low : low + BLOCK, :].astype(jnp.bfloat16)
                part_copy(u, t, d).start()
        for t in range(2):
            pre_out[u, t] = acc[t, 0:PREFIX, :].astype(jnp.bfloat16)
            own_sum[u, t] = acc[t, OWN:KEYS, :]

        @pl.when(a == u)
        def _():
            pre_in[here] = pre_out[u, :, piece_rows(s), :]

        @pl.when(a != u)
        def _():
            pre_copy(u, 0).start()

        def spread(i, carry):
            pre_copy(u, i).start()
            return carry

        lax.fori_loop(1, SEQ, spread, 0)

    def finish(u):
        for t in (1, 0):
            wait_for(part_in.at[u, t], part_recv.at[u, t])
            whole = own_sum[u, t]
            for d in steps_back:
                whole += part_in[u, t, d - 1].astype(jnp.float32)
            if t == 0:
                whole = whole * SCALE
            own_out[u, t] = whole.astype(jnp.bfloat16)
            for j in (2, 1, 3):
                own_copy(u, t, j).start()
            own_own(u, t).start()

    def hand_prefix(u):
        @pl.when(a == u)
        def _():
            wait_for(pre_in.at[0 : BLOCKS - 1], pre_recv.at[0])
            for t in range(2):
                whole = jnp.sum(pre_in[:, t].astype(jnp.float32), axis=0)
                if t == 0:
                    whole = whole * SCALE
                pre_sum[t] = whole.astype(jnp.bfloat16)
            for t in range(2):
                for i in range(1, SEQ):
                    last_copy(t, i).start()
                last_own(t).start()

    wait_for(kv.at[0, :, 0:PREFIX], fix_local.at[0])
    wait_for(kv.at[0, :, 0:PREFIX], fix_recv.at[0])

    def step(n, carry):
        u = n // PARTS

        @pl.when(n == 0)
        def _():
            send_windows(1)

        @pl.when(lax.rem(n, PARTS) == 0)
        def _():
            prepare(u)

        wait_for(xb.at[n], in_recv.at[n])

        attend(n, u)

        @pl.when(lax.rem(n, PARTS) == PARTS - 1)
        def _():
            close(u)

        @pl.when(n == PARTS - 1)
        def _():
            query_part(0)

        @pl.when(n == PARTS)
        def _():
            finish(0)
            hand_prefix(0)

        return carry

    lax.fori_loop(0, STEPS, step, 0)

    query_part(1)
    hand_prefix(1)
    finish(1)

    for t in range(2):
        wait_for(xb.at[0:3, t], in_send.at[t])
        wait_for((dk, dv)[t], own_recv.at[t])
        wait_for((dpk, dpv)[t], last_recv.at[t])
    wait_for(dqb.at[0:3], dq_send.at[0])
    wait_for(dq, dq_recv.at[0])
    wait_for(own_out.at[:, :, 0 : BLOCK - ROWS], kv_send.at[0])
    wait_for(own_out.at[:, :, 0 : BLOCK - ROWS], own_send.at[0])
    wait_for(pre_out.at[0], fix_send.at[0])
    wait_for(pre_out.at[0, :, 0 : PREFIX - PIECE], last_send.at[0])
    wait_for(pre_in.at[0 : BLOCKS - 1], pre_send.at[0])
    for u in range(SLOTS):
        wait_for(kv.at[u, :, PREFIX:OWN, :], win_send.at[u])
        for t in range(2):
            wait_for(part_out.at[u, t], part_send.at[u, t])


def hand_over(*refs):
    count = (len(refs) - 2) // 3
    before, after, held = refs[:count], refs[count : 2 * count], refs[2 * count : 3 * count]
    arrived, stored = refs[-2:]
    pieces = []
    for i in range(count):
        rows = before[i].shape[0]
        size = 16 if before[i].shape[1] > GROUP else rows
        for first in range(0, rows, size):
            n = len(pieces)
            part = pl.ds(first, size)
            pieces.append(
                (
                    pltpu.make_async_copy(before[i].at[part], held[i].at[part], arrived.at[n]),
                    pltpu.make_async_copy(held[i].at[part], after[i].at[part], stored.at[n]),
                )
            )
    for load, store in pieces:
        load.start()
    for load, store in pieces:
        load.wait()
        store.start()
    for load, store in pieces:
        store.wait()


def on_device(queries, keys, values, out_grad, prefix_keys, prefix_values, seg_ids, prefix_lens):
    bf16, f32 = jnp.bfloat16, jnp.float32
    dma = pltpu.SemaphoreType.DMA
    hbm = pl.BlockSpec(memory_space=pl.ANY)
    arrays = [
        ((STEPS, 2, BLOCK, WIDE), bf16),
        ((SLOTS, 2, KEYS, HEAD_DIM), bf16),
        ((KEYS, 128), bf16),
        ((BLOCK, 128), bf16),
        ((HEAD_DIM, KEYS), bf16),
        ((2, KEYS, HEAD_DIM), f32),
        ((SLOTS, 2, BLOCK, HEAD_DIM), f32),
        ((SPAN, WIDE), f32),
        ((SPAN, WIDE), f32),
        ((SPAN, WIDE), bf16),
        ((SPAN, GROUP), bf16),
        ((SPAN, WIDE), f32),
        ((SPAN, WIDE), f32),
        ((SPAN, WIDE), bf16),
        ((SPAN, GROUP), bf16),
        ((STEPS, BLOCK, WIDE), bf16),
        ((SLOTS, 2, BACK, BLOCK, HEAD_DIM), bf16),
        ((SLOTS, 2, BACK, BLOCK, HEAD_DIM), bf16),
        ((SLOTS, 2, BLOCK, HEAD_DIM), bf16),
        ((SLOTS, 2, PREFIX, HEAD_DIM), bf16),
        ((BLOCKS, 2, PIECE, HEAD_DIM), bf16),
        ((2, PIECE, HEAD_DIM), bf16),
    ]
    semaphores = [
        2,
        1,
        SLOTS,
        1,
        1,
        1,
        SLOTS,
        SLOTS,
        2,
        STEPS,
        1,
        1,
        (SLOTS, 2),
        (SLOTS, 2),
        1,
        2,
        1,
        1,
        1,
        2,
    ]
    results = (
        jax.ShapeDtypeStruct(queries.shape, bf16),
        jax.ShapeDtypeStruct(keys.shape, bf16),
        jax.ShapeDtypeStruct(values.shape, bf16),
        jax.ShapeDtypeStruct(prefix_keys.shape, bf16),
        jax.ShapeDtypeStruct(prefix_values.shape, bf16),
    )
    raw = pl.pallas_call(
        kernel,
        out_shape=results,
        in_specs=[hbm] * 8,
        out_specs=(hbm,) * 5,
        scratch_shapes=[pltpu.VMEM(shape, kind) for shape, kind in arrays]
        + [pltpu.VMEM((64, 128), jnp.int32), pltpu.SMEM((SEGS,), jnp.int32)]
        + [dma(size if isinstance(size, tuple) else (size,)) for size in semaphores],
        compiler_params=pltpu.CompilerParams(
            collective_id=0, has_side_effects=True, vmem_limit_bytes=56 * 1024 * 1024
        ),
        cost_estimate=pl.CostEstimate(
            flops=4096 * SPAN * HEAD_DIM * 10,
            bytes_accessed=4 * 1024 * 1024,
            transcendentals=4096 * SPAN,
        ),
    )(
        queries,
        out_grad,
        keys,
        values,
        prefix_keys,
        prefix_values,
        seg_ids.reshape(64, 128),
        prefix_lens,
    )
    return pl.pallas_call(
        hand_over,
        out_shape=results,
        in_specs=[hbm] * len(results),
        out_specs=(hbm,) * len(results),
        scratch_shapes=[pltpu.VMEM(x.shape, x.dtype) for x in results] + [dma((16,)), dma((16,))],
    )(*raw)


def solution(mesh):
    return jax.shard_map(
        on_device,
        mesh=mesh,
        in_specs=(
            P(("seq", "head"), None),
            P(("seq", "head"), None),
            P(("seq", "head"), None),
            P(("seq", "head"), None),
            P(None, "head"),
            P(None, "head"),
            P(),
            P(),
        ),
        out_specs=(
            P(("seq", "head"), None),
            P(("seq", "head"), None),
            P(("seq", "head"), None),
            P(None, "head"),
            P(None, "head"),
        ),
        check_vma=False,
    )
```

```python
import math

import jax
import jax.numpy as jnp
from jax import lax
from jax.experimental import pallas as pl
from jax.experimental.pallas import tpu as pltpu
from jax.sharding import PartitionSpec as P

MESH = pl.DeviceIdType.MESH

HEAD_DIM = 128
PREFIX = 256
RING = 4
ROWS = 64
BLOCK = RING * ROWS
BACK = 4
WINDOW = (BACK + 1) * BLOCK
KEYS = PREFIX + WINDOW
OWN = PREFIX + BACK * BLOCK
SLOTS = 2
HEADS = 4
PARTS = 2
STEPS = SLOTS * PARTS
WIDE = HEADS * HEAD_DIM
GROUP = PARTS * WIDE
SUB = 128
NEAR = 1024 + SUB
SPAN = PREFIX + NEAR
TILE = 128
HALF = 256
CUTS = [(0, PREFIX)] + [(PREFIX + NEAR // 3 * i, NEAR // 3) for i in range(3)]
BLOCKS = 32
SEQ = 16
SEGS = 32
SCALE = HEAD_DIM**-0.5
EXP_SCALE = SCALE / math.log(2.0)
MASKED = -1e30
PIECE = PREFIX // SEQ


def dot_nt(a, b):
    return lax.dot_general(a, b, (((1,), (1,)), ((), ())), preferred_element_type=jnp.float32)


def dot_nn(a, b):
    return lax.dot_general(a, b, (((1,), (0,)), ((), ())), preferred_element_type=jnp.float32)


def kernel(
    q,
    g,
    k,
    v,
    pk,
    pv,
    seg_hbm,
    lens_hbm,
    dq,
    dk,
    dv,
    dpk,
    dpv,
    xb,
    kv,
    ext,
    qx,
    kt,
    acc,
    own_sum,
    s_0,
    d_0,
    p_0,
    ds_0,
    s_1,
    d_1,
    p_1,
    ds_1,
    dqb,
    part_out,
    part_in,
    merge_in,
    own_out,
    pre_out,
    pre_in,
    pre_sum,
    seg,
    lens,
    small_sem,
    kv_send,
    kv_recv,
    fix_local,
    fix_send,
    fix_recv,
    win_send,
    win_recv,
    in_send,
    in_recv,
    dq_send,
    dq_recv,
    part_send,
    part_recv,
    merge_recv,
    own_send,
    own_recv,
    pre_send,
    pre_recv,
    last_send,
    last_recv,
):
    s = lax.axis_index("seq")
    h = lax.axis_index("head")
    y = lax.rem(h, RING)
    a = h // RING
    here = 2 * s + a
    place = lax.rem(here, 4)
    first_core = place < 2

    def at_y(j):
        return (s, RING * a + lax.rem(y + j, RING))

    def at_block(b):
        return (b // 2, lax.rem(b, 2) * RING + y)

    def columns(first, size):
        return pl.ds(pl.multiple_of(first, 128), size)

    def rows_of(j):
        return pl.ds(pl.multiple_of(ROWS * j, ROWS), ROWS)

    def remote(src, dst, send, recv, device):
        return pltpu.make_async_remote_copy(
            src_ref=src,
            dst_ref=dst,
            send_sem=send,
            recv_sem=recv,
            device_id=device,
            device_id_type=MESH,
        )

    small = [
        pltpu.make_async_copy(seg_hbm, seg, small_sem.at[0]),
        pltpu.make_async_copy(lens_hbm, lens, small_sem.at[1]),
    ]
    for copy in small:
        copy.start()

    def wait_for(ref, sem):
        pltpu.make_async_copy(ref, ref, sem).wait()

    barrier = pltpu.get_barrier_semaphore()
    for j in range(1, RING):
        pl.semaphore_signal(barrier, inc=1, device_id=at_y(j), device_id_type=MESH)

    def greet(d, carry):
        there = at_block(lax.rem(here + d, BLOCKS))
        pl.semaphore_signal(barrier, inc=1, device_id=there, device_id_type=MESH)
        return carry

    lax.fori_loop(1, BLOCKS, greet, 0)
    def kv_own(u, t):
        src = (k, v)[t].at[:, columns((RING * u + y) * HEAD_DIM, HEAD_DIM)]
        dst = kv.at[u, t, pl.ds(pl.multiple_of(OWN + ROWS * y, ROWS), ROWS)]
        return pltpu.make_async_copy(src, dst, kv_recv.at[u])

    def kv_copy(u, t, j):
        there = lax.rem(y + j, RING)
        src = (k, v)[t].at[:, columns((RING * u + there) * HEAD_DIM, HEAD_DIM)]
        dst = kv.at[u, t, pl.ds(pl.multiple_of(OWN + ROWS * y, ROWS), ROWS)]
        return remote(src, dst, kv_send.at[0], kv_recv.at[u], at_y(j))

    def fix_own(t):
        return pltpu.make_async_copy((pk, pv)[t], kv.at[a, t, 0:PREFIX], fix_local.at[0])

    def fix_copy(t):
        device = (s, RING * (1 - a) + y)
        return remote(
            (pk, pv)[t], kv.at[a, t, 0:PREFIX], fix_send.at[0], fix_recv.at[0], device
        )

    def win_copy(u, d):
        src = kv.at[u, :, OWN:KEYS, :]
        dst = kv.at[u, :, OWN - d * BLOCK : KEYS - d * BLOCK, :]
        device = at_block(lax.rem(here + d, BLOCKS))
        return remote(src, dst, win_send.at[u], win_recv.at[u, (d - 1) // 2], device)

    def win_share(u):
        src = kv.at[u, :, OWN - 2 * BLOCK : OWN, :]
        dst = kv.at[u, :, OWN - 4 * BLOCK : OWN - 2 * BLOCK, :]
        return remote(src, dst, win_send.at[u], win_recv.at[u, 1], at_block(here + 2))

    def in_first(n, there):
        return (RING * (n // PARTS) + there) * GROUP + lax.rem(n, PARTS) * WIDE

    def in_own(n, t):
        src = (q, g)[t].at[:, columns(in_first(n, y), WIDE)]
        return pltpu.make_async_copy(src, xb.at[n, t, rows_of(y)], in_recv.at[n])

    def in_copy(n, t, j):
        src = (q, g)[t].at[:, columns(in_first(n, lax.rem(y + j, RING)), WIDE)]
        return remote(src, xb.at[n, t, rows_of(y)], in_send.at[t], in_recv.at[n], at_y(j))

    def dq_own(n):
        dst = dq.at[:, columns(in_first(n, y), WIDE)]
        return pltpu.make_async_copy(dqb.at[n, rows_of(y)], dst, dq_recv.at[0])

    def dq_copy(n, j):
        src = dqb.at[n, rows_of(lax.rem(y + j, RING))]
        dst = dq.at[:, columns(in_first(n, y), WIDE)]
        return remote(src, dst, dq_send.at[0], dq_recv.at[0], at_y(j))

    def part_copy(u, t, d):
        device = at_block(lax.rem(here + BLOCKS - d, BLOCKS))
        return remote(
            part_out.at[u, t, d - 1],
            part_in.at[u, t, d - 1],
            part_send.at[u, t],
            part_recv.at[u, t],
            device,
        )

    def merge_copy(u, t):
        device = at_block(lax.rem(here + BLOCKS - 2, BLOCKS))
        return remote(
            part_out.at[u, t, 2:4],
            merge_in.at[u, t],
            part_send.at[u, t],
            merge_recv.at[u, t],
            device,
        )

    def own_own(u, t):
        dst = (dk, dv)[t].at[:, columns((RING * u + y) * HEAD_DIM, HEAD_DIM)]
        return pltpu.make_async_copy(own_out.at[u, t, rows_of(y)], dst, own_recv.at[t])

    def own_copy(u, t, j):
        src = own_out.at[u, t, rows_of(lax.rem(y + j, RING))]
        dst = (dk, dv)[t].at[:, columns((RING * u + y) * HEAD_DIM, HEAD_DIM)]
        return remote(src, dst, own_send.at[0], own_recv.at[t], at_y(j))

    def piece_rows(r):
        return pl.ds(pl.multiple_of(PIECE * r, PIECE), PIECE)

    def pre_copy(u, i):
        r = lax.rem(s + i, SEQ)
        return remote(
            pre_out.at[u, :, piece_rows(r)],
            pre_in.at[here],
            pre_send.at[0],
            pre_recv.at[0],
            (r, RING * u + y),
        )

    def last_own(t):
        return pltpu.make_async_copy(
            pre_sum.at[t], (dpk, dpv)[t].at[piece_rows(s)], last_recv.at[t]
        )

    def last_copy(t, i):
        return remote(
            pre_sum.at[t],
            (dpk, dpv)[t].at[piece_rows(s)],
            last_send.at[0],
            last_recv.at[t],
            (lax.rem(s + i, SEQ), h),
        )

    others = range(1, RING)
    steps_back = range(1, BACK + 1)

    def send_in(n):
        for t in range(2):
            for j in (2, 1, 3):
                in_copy(n, t, j).start()

    def send_kv(u):
        for t in range(2):
            for j in (2, 1, 3):
                kv_copy(u, t, j).start()

    def send_windows(u):
        wait_for(kv.at[u, :, OWN:KEYS, :], kv_recv.at[u])
        win_copy(u, 1).start()
        win_copy(u, 2).start()

        @pl.when((place == 1) | (place == 2))
        def _():
            win_copy(u, 3).start()

        @pl.when(first_core)
        def _():
            win_copy(u, 4).start()

    def share_windows(u):
        wait_for(kv.at[u, :, OWN - 2 * BLOCK : OWN, :], win_recv.at[u, 0])

        @pl.when(first_core)
        def _():
            win_share(u).start()

    for t in range(2):
        for u in range(SLOTS):
            kv_own(u, t).start()
        fix_own(t).start()
    for n in range(STEPS):
        for t in range(2):
            in_own(n, t).start()

    for copy in small:
        copy.wait()
    @pl.when((place == 0) | (place == 3))
    def _():
        part_in[:, :, 2] = jnp.zeros((SLOTS, 2, BLOCK, HEAD_DIM), jnp.bfloat16)

    @pl.when(jnp.logical_not(first_core))
    def _():
        part_in[:, :, 3] = jnp.zeros((SLOTS, 2, BLOCK, HEAD_DIM), jnp.bfloat16)

    documents = lax.broadcasted_iota(jnp.int32, (128, 128), 0)
    limits = jnp.zeros((128, 128), jnp.int32)
    for e in range(SEGS):
        limits = jnp.where(documents == e, lens[e], limits)
    lanes = lax.broadcasted_iota(jnp.int32, (128, 128), 1)
    for i in range(PREFIX // 128):
        hidden = jnp.where(lanes + 128 * i < limits, 0.0, MASKED)
        ext[128 * i : 128 * (i + 1), :] = hidden.T.astype(jnp.bfloat16)
    for i in range(WINDOW // 128):
        row = 2 * here - 2 * BACK + i
        names = jnp.broadcast_to(seg[pl.ds(jnp.maximum(row, 0), 1), :], (128, 128))
        real = jnp.full((128, 128), row, jnp.int32) >= 0
        hidden = jnp.where((names == documents) & real, 0.0, MASKED)
        ext[PREFIX + 128 * i : PREFIX + 128 * (i + 1), :] = hidden.T.astype(jnp.bfloat16)
        if i >= 2 * BACK:
            picked = jnp.where(names == documents, 1.0, 0.0)
            first = 128 * (i - 2 * BACK)
            qx[first : first + 128, :] = picked.T.astype(jnp.bfloat16)

    pl.semaphore_wait(barrier, RING - 1 + BLOCKS - 1)
    send_kv(0)
    for t in range(2):
        fix_copy(t).start()
    send_in(0)
    send_kv(1)

    send_windows(0)
    for n in range(1, STEPS):
        send_in(n)

    def prepare(u):
        wait_for(kv.at[u, :, PREFIX : OWN - 2 * BLOCK, :], win_recv.at[u, 1])
        for i in range(KEYS // 128):
            part = kv[u, 0, 128 * i : 128 * (i + 1), :].astype(jnp.float32)
            kt[:, 128 * i : 128 * (i + 1)] = part.T.astype(jnp.bfloat16)
        acc[...] = jnp.zeros_like(acc)

    passes = ((s_0, d_0, p_0, ds_0), (s_1, d_1, p_1, ds_1))

    def key_rows(i, cut):
        first, size = cut
        return pl.ds(first if first < PREFIX else first + SUB * i, size)

    def load_rows(n, t, i):
        rows = pl.ds(SUB * i, SUB)
        return jnp.concatenate(
            [xb[n, t, rows, HEAD_DIM * x : HEAD_DIM * (x + 1)] for x in range(HEADS)], axis=0
        )

    def score(u, i, q2, g2):
        s_ref, d_ref, _, _ = passes[i]
        marks = jnp.concatenate([qx[pl.ds(SUB * i, SUB), :]] * HEADS, axis=0)
        q_wide = jnp.concatenate([q2, marks], axis=1)

        def keys(cut):
            rows = key_rows(i, cut)
            wide = jnp.concatenate([kv[u, 0, rows, :], ext[rows, :]], axis=1)
            s_ref[pl.ds(*cut), :] = dot_nt(wide, q_wide)

        def values(cut):
            d_ref[pl.ds(*cut), :] = dot_nt(kv[u, 1, key_rows(i, cut), :], g2)

        for cut in CUTS:
            yield lambda: keys(cut)
        for cut in CUTS:
            yield lambda: values(cut)

    def weigh(i, first):
        s_ref, d_ref, p_ref, ds_ref = passes[i]
        tiles = [pl.ds(f, TILE) for f in range(0, SPAN, TILE)]
        key_at = lax.broadcasted_iota(jnp.int32, (SUB, HALF), 0)
        row_at = lax.rem(lax.broadcasted_iota(jnp.int32, (SUB, HALF), 1), SUB)

        def fold(tile):
            return tile.reshape(TILE // 8, 8, HALF)

        for c in range(0, WIDE, HALF):
            cols = pl.ds(c, HALF)
            out = pl.ds(pl.multiple_of(first + c, HALF), HALF)
            has = {}

            def begin():
                last = pl.ds(SPAN - SUB, SUB)
                s_ref[last, cols] = jnp.where(key_at <= row_at, s_ref[last, cols], MASKED)
                has["peak"] = jnp.full((8, HALF), MASKED, jnp.float32)
                has["total"] = jnp.zeros((8, HALF), jnp.float32)
                has["weighted"] = jnp.zeros((8, HALF), jnp.float32)

            def top(tile):
                has["peak"] = jnp.maximum(has["peak"], jnp.max(fold(s_ref[tile, cols]), axis=0))

            def level():
                has["peak"] = jnp.max(has["peak"], axis=0, keepdims=True)

            def weight(tile):
                weights = jnp.exp2((s_ref[tile, cols] - has["peak"]) * EXP_SCALE)
                s_ref[tile, cols] = weights
                has["total"] += jnp.sum(fold(weights), axis=0)
                has["weighted"] += jnp.sum(fold(weights * d_ref[tile, cols]), axis=0)

            def settle():
                has["inverse"] = 1.0 / jnp.sum(has["total"], axis=0, keepdims=True)
                weighted = jnp.sum(has["weighted"], axis=0, keepdims=True)
                has["delta"] = weighted * has["inverse"]

            def grade(tile):
                probs = s_ref[tile, cols] * has["inverse"]
                p_ref[tile, cols] = probs.astype(jnp.bfloat16)
                score_grad = probs * (d_ref[tile, cols] - has["delta"])
                ds_ref[tile, out] = score_grad.astype(jnp.bfloat16)

            yield begin
            for tile in tiles:
                yield lambda: top(tile)
            yield level
            for tile in tiles:
                yield lambda: weight(tile)
            yield settle
            for tile in tiles:
                yield lambda: grade(tile)

    def gather_up(i, first, q2, g2):
        _, _, p_ref, ds_ref = passes[i]
        cols = pl.ds(pl.multiple_of(first, WIDE), WIDE)

        def values(cut):
            acc[1, key_rows(i, cut), :] += dot_nn(p_ref[pl.ds(*cut), :], g2)

        def keys(cut):
            acc[0, key_rows(i, cut), :] += dot_nn(ds_ref[pl.ds(*cut), cols], q2)

        for cut in CUTS:
            yield lambda: values(cut)
        for cut in CUTS:
            yield lambda: keys(cut)

    def together(products, count, others, other_count):
        done = 0
        for i in range(other_count):
            while done < count and done * other_count <= i * count:
                next(products)()
                done += 1
            next(others)()
        for rest in products:
            rest()

    def attend(n, u):
        first = lax.rem(n, PARTS) * WIDE
        held = [[load_rows(n, t, i) for t in range(2)] for i in range(2)]
        products = 2 * len(CUTS)
        passing = WIDE // HALF * (3 * (SPAN // TILE) + 3)
        for do in score(u, 0, *held[0]):
            do()
        together(score(u, 1, *held[1]), products, weigh(0, first), passing)
        together(gather_up(0, first, *held[0]), products, weigh(1, first), passing)
        for do in gather_up(1, first, *held[1]):
            do()

    def query_part(u):
        for i in range(2):
            _, _, _, ds_ref = passes[i]
            rows = pl.ds(SUB * i, SUB)
            near = pl.ds(PREFIX + SUB * i, NEAR)
            grad = dot_nn(kt[:, 0:PREFIX], ds_ref[0:PREFIX, :])
            grad += dot_nn(kt[:, near], ds_ref[PREFIX:SPAN, :])
            grad = (grad * SCALE).T.astype(jnp.bfloat16)
            for x in range(PARTS * HEADS):
                cols = pl.ds(HEAD_DIM * (x % HEADS), HEAD_DIM)
                dqb[PARTS * u + x // HEADS, rows, cols] = grad[SUB * x : SUB * (x + 1)]
        for n in range(PARTS):
            for j in (2, 1, 3):
                dq_copy(PARTS * u + n, j).start()
            dq_own(PARTS * u + n).start()

    def close(u):
        for t in (1, 0):
            for d in (3, 4, 1, 2):
                low = OWN - d * BLOCK
                part_out[u, t, d - 1] = acc[t, low : low + BLOCK, :].astype(jnp.bfloat16)

            @pl.when(first_core)
            def _():
                part_copy(u, t, 3).start()
                part_copy(u, t, 4).start()

            @pl.when(jnp.logical_not(first_core))
            def _():
                merge_copy(u, t).start()
                part_copy(u, t, 1).start()
                part_copy(u, t, 2).start()

        for t in range(2):
            pre_out[u, t] = acc[t, 0:PREFIX, :].astype(jnp.bfloat16)
            own_sum[u, t] = acc[t, OWN:KEYS, :]

        @pl.when(a == u)
        def _():
            pre_in[here] = pre_out[u, :, piece_rows(s), :]

        @pl.when(a != u)
        def _():
            pre_copy(u, 0).start()

        def spread(i, carry):
            pre_copy(u, i).start()
            return carry

        lax.fori_loop(1, SEQ, spread, 0)

    def merge(u):
        @pl.when(first_core)
        def _():
            for t in (1, 0):
                wait_for(merge_in.at[u, t], merge_recv.at[u, t])
                for d in (1, 2):
                    both = part_out[u, t, d - 1].astype(jnp.float32)
                    both += merge_in[u, t, d - 1].astype(jnp.float32)
                    part_out[u, t, d - 1] = both.astype(jnp.bfloat16)
                    part_copy(u, t, d).start()

    def finish(u):
        for t in (1, 0):
            for at, count in enumerate((3, 4, 3, 2)):

                @pl.when(place == at)
                def _():
                    wait_for(part_in.at[u, t, 0:count], part_recv.at[u, t])

            whole = own_sum[u, t]
            for d in steps_back:
                whole += part_in[u, t, d - 1].astype(jnp.float32)
            if t == 0:
                whole = whole * SCALE
            own_out[u, t] = whole.astype(jnp.bfloat16)
            for j in (2, 1, 3):
                own_copy(u, t, j).start()
            own_own(u, t).start()

    def hand_prefix(u):
        @pl.when(a == u)
        def _():
            wait_for(pre_in.at[0 : BLOCKS - 1], pre_recv.at[0])
            for t in range(2):
                whole = jnp.sum(pre_in[:, t].astype(jnp.float32), axis=0)
                if t == 0:
                    whole = whole * SCALE
                pre_sum[t] = whole.astype(jnp.bfloat16)
            for t in range(2):
                for i in range(1, SEQ):
                    last_copy(t, i).start()
                last_own(t).start()

    wait_for(kv.at[0, :, 0:PREFIX], fix_local.at[0])
    wait_for(kv.at[0, :, 0:PREFIX], fix_recv.at[0])

    def step(n, carry):
        u = n // PARTS

        @pl.when(n == 0)
        def _():
            send_windows(1)
            share_windows(0)

        @pl.when(lax.rem(n, PARTS) == 0)
        def _():
            prepare(u)

        wait_for(xb.at[n], in_recv.at[n])

        attend(n, u)

        @pl.when(n == PARTS - 1)
        def _():
            share_windows(1)

        @pl.when(lax.rem(n, PARTS) == PARTS - 1)
        def _():
            close(u)

        @pl.when(n == PARTS - 1)
        def _():
            query_part(0)

        @pl.when(n == PARTS - 1)
        def _():
            merge(0)

        @pl.when(n == PARTS)
        def _():
            finish(0)
            hand_prefix(0)

        return carry

    lax.fori_loop(0, STEPS, step, 0)

    merge(1)
    query_part(1)
    hand_prefix(1)
    finish(1)

    for t in range(2):
        wait_for(xb.at[0:3, t], in_send.at[t])
        wait_for((dk, dv)[t], own_recv.at[t])
        wait_for((dpk, dpv)[t], last_recv.at[t])
    wait_for(dqb.at[0:3], dq_send.at[0])
    wait_for(dq, dq_recv.at[0])
    wait_for(own_out.at[:, :, 0 : BLOCK - ROWS], kv_send.at[0])
    wait_for(own_out.at[:, :, 0 : BLOCK - ROWS], own_send.at[0])
    wait_for(pre_out.at[0], fix_send.at[0])
    wait_for(pre_out.at[0, :, 0 : PREFIX - PIECE], last_send.at[0])
    wait_for(pre_in.at[0 : BLOCKS - 1], pre_send.at[0])
    for u in range(SLOTS):
        for at, sent in enumerate((5, 6, 3, 2)):

            @pl.when(place == at)
            def _():
                wait_for(kv.at[u, :, 0 : sent * BLOCK, :], win_send.at[u])

        for t in range(2):
            wait_for(part_out.at[u, t], part_send.at[u, t])


def hand_over(*refs):
    count = (len(refs) - 2) // 3
    before, after, held = refs[:count], refs[count : 2 * count], refs[2 * count : 3 * count]
    arrived, stored = refs[-2:]
    pieces = []
    for i in range(count):
        rows = before[i].shape[0]
        size = 16 if before[i].shape[1] > GROUP else rows
        for first in range(0, rows, size):
            n = len(pieces)
            part = pl.ds(first, size)
            pieces.append(
                (
                    pltpu.make_async_copy(before[i].at[part], held[i].at[part], arrived.at[n]),
                    pltpu.make_async_copy(held[i].at[part], after[i].at[part], stored.at[n]),
                )
            )
    for load, store in pieces:
        load.start()
    for load, store in pieces:
        load.wait()
        store.start()
    for load, store in pieces:
        store.wait()


def on_device(queries, keys, values, out_grad, prefix_keys, prefix_values, seg_ids, prefix_lens):
    bf16, f32 = jnp.bfloat16, jnp.float32
    dma = pltpu.SemaphoreType.DMA
    hbm = pl.BlockSpec(memory_space=pl.ANY)
    arrays = [
        ((STEPS, 2, BLOCK, WIDE), bf16),
        ((SLOTS, 2, KEYS, HEAD_DIM), bf16),
        ((KEYS, 128), bf16),
        ((BLOCK, 128), bf16),
        ((HEAD_DIM, KEYS), bf16),
        ((2, KEYS, HEAD_DIM), f32),
        ((SLOTS, 2, BLOCK, HEAD_DIM), f32),
        ((SPAN, WIDE), f32),
        ((SPAN, WIDE), f32),
        ((SPAN, WIDE), bf16),
        ((SPAN, GROUP), bf16),
        ((SPAN, WIDE), f32),
        ((SPAN, WIDE), f32),
        ((SPAN, WIDE), bf16),
        ((SPAN, GROUP), bf16),
        ((STEPS, BLOCK, WIDE), bf16),
        ((SLOTS, 2, BACK, BLOCK, HEAD_DIM), bf16),
        ((SLOTS, 2, BACK, BLOCK, HEAD_DIM), bf16),
        ((SLOTS, 2, 2, BLOCK, HEAD_DIM), bf16),
        ((SLOTS, 2, BLOCK, HEAD_DIM), bf16),
        ((SLOTS, 2, PREFIX, HEAD_DIM), bf16),
        ((BLOCKS, 2, PIECE, HEAD_DIM), bf16),
        ((2, PIECE, HEAD_DIM), bf16),
    ]
    semaphores = [
        2,
        1,
        SLOTS,
        1,
        1,
        1,
        SLOTS,
        (SLOTS, 2),
        2,
        STEPS,
        1,
        1,
        (SLOTS, 2),
        (SLOTS, 2),
        (SLOTS, 2),
        1,
        2,
        1,
        1,
        1,
        2,
    ]
    results = (
        jax.ShapeDtypeStruct(queries.shape, bf16),
        jax.ShapeDtypeStruct(keys.shape, bf16),
        jax.ShapeDtypeStruct(values.shape, bf16),
        jax.ShapeDtypeStruct(prefix_keys.shape, bf16),
        jax.ShapeDtypeStruct(prefix_values.shape, bf16),
    )
    raw = pl.pallas_call(
        kernel,
        out_shape=results,
        in_specs=[hbm] * 8,
        out_specs=(hbm,) * 5,
        scratch_shapes=[pltpu.VMEM(shape, kind) for shape, kind in arrays]
        + [pltpu.VMEM((64, 128), jnp.int32), pltpu.SMEM((SEGS,), jnp.int32)]
        + [dma(size if isinstance(size, tuple) else (size,)) for size in semaphores],
        compiler_params=pltpu.CompilerParams(
            collective_id=0, has_side_effects=True, vmem_limit_bytes=56 * 1024 * 1024
        ),
        cost_estimate=pl.CostEstimate(
            flops=4096 * SPAN * HEAD_DIM * 10,
            bytes_accessed=4 * 1024 * 1024,
            transcendentals=4096 * SPAN,
        ),
    )(
        queries,
        out_grad,
        keys,
        values,
        prefix_keys,
        prefix_values,
        seg_ids.reshape(64, 128),
        prefix_lens,
    )
    return pl.pallas_call(
        hand_over,
        out_shape=results,
        in_specs=[hbm] * len(results),
        out_specs=(hbm,) * len(results),
        scratch_shapes=[pltpu.VMEM(x.shape, x.dtype) for x in results] + [dma((16,)), dma((16,))],
    )(*raw)


def solution(mesh):
    return jax.shard_map(
        on_device,
        mesh=mesh,
        in_specs=(
            P(("seq", "head"), None),
            P(("seq", "head"), None),
            P(("seq", "head"), None),
            P(("seq", "head"), None),
            P(None, "head"),
            P(None, "head"),
            P(),
            P(),
        ),
        out_specs=(
            P(("seq", "head"), None),
            P(("seq", "head"), None),
            P(("seq", "head"), None),
            P(None, "head"),
            P(None, "head"),
        ),
        check_vma=False,
    )
```

```python
import math

import jax
import jax.numpy as jnp
from jax import lax
from jax.experimental import pallas as pl
from jax.experimental.pallas import tpu as pltpu
from jax.sharding import PartitionSpec as P

MESH = pl.DeviceIdType.MESH

HEAD_DIM = 128
PREFIX = 256
RING = 4
ROWS = 64
BLOCK = RING * ROWS
BACK = 4
WINDOW = (BACK + 1) * BLOCK
KEYS = PREFIX + WINDOW
OWN = PREFIX + BACK * BLOCK
SLOTS = 2
HEADS = 4
PARTS = 2
STEPS = SLOTS * PARTS
WIDE = HEADS * HEAD_DIM
GROUP = PARTS * WIDE
SUB = 128
NEAR = 1024 + SUB
SPAN = PREFIX + NEAR
TILE = 128
HALF = 256
CUTS = [(0, PREFIX)] + [(PREFIX + NEAR // 3 * i, NEAR // 3) for i in range(3)]
BLOCKS = 32
SEQ = 16
SEGS = 32
SCALE = HEAD_DIM**-0.5
EXP_SCALE = SCALE / math.log(2.0)
MASKED = -1e30
PIECE = PREFIX // SEQ


def dot_nt(a, b):
    return lax.dot_general(a, b, (((1,), (1,)), ((), ())), preferred_element_type=jnp.float32)


def dot_nn(a, b):
    return lax.dot_general(a, b, (((1,), (0,)), ((), ())), preferred_element_type=jnp.float32)


def kernel(
    q,
    g,
    k,
    v,
    pk,
    pv,
    seg_hbm,
    lens_hbm,
    dq,
    dk,
    dv,
    dpk,
    dpv,
    xb,
    kv,
    ext,
    qx,
    kt,
    acc,
    own_sum,
    s_0,
    d_0,
    p_0,
    ds_0,
    s_1,
    d_1,
    p_1,
    ds_1,
    dqb,
    part_out,
    part_in,
    merge_in,
    own_out,
    pre_out,
    pre_in,
    pre_sum,
    seg,
    lens,
    small_sem,
    kv_send,
    kv_recv,
    fix_local,
    fix_send,
    fix_recv,
    win_send,
    win_recv,
    in_send,
    in_recv,
    dq_send,
    dq_recv,
    part_send,
    part_recv,
    merge_recv,
    own_send,
    own_recv,
    pre_send,
    pre_recv,
    last_send,
    last_recv,
):
    s = lax.axis_index("seq")
    h = lax.axis_index("head")
    y = lax.rem(h, RING)
    a = h // RING
    here = 2 * s + a
    place = lax.rem(here, 4)
    first_core = place < 2

    def at_y(j):
        return (s, RING * a + lax.rem(y + j, RING))

    def at_block(b):
        return (b // 2, lax.rem(b, 2) * RING + y)

    def columns(first, size):
        return pl.ds(pl.multiple_of(first, 128), size)

    def rows_of(j):
        return pl.ds(pl.multiple_of(ROWS * j, ROWS), ROWS)

    def remote(src, dst, send, recv, device):
        return pltpu.make_async_remote_copy(
            src_ref=src,
            dst_ref=dst,
            send_sem=send,
            recv_sem=recv,
            device_id=device,
            device_id_type=MESH,
        )

    small = [
        pltpu.make_async_copy(seg_hbm, seg, small_sem.at[0]),
        pltpu.make_async_copy(lens_hbm, lens, small_sem.at[1]),
    ]
    for copy in small:
        copy.start()

    def wait_for(ref, sem):
        pltpu.make_async_copy(ref, ref, sem).wait()

    barrier = pltpu.get_barrier_semaphore()
    for j in range(1, RING):
        pl.semaphore_signal(barrier, inc=1, device_id=at_y(j), device_id_type=MESH)

    def greet(d, carry):
        there = at_block(lax.rem(here + d, BLOCKS))
        pl.semaphore_signal(barrier, inc=1, device_id=there, device_id_type=MESH)
        return carry

    lax.fori_loop(1, BLOCKS, greet, 0)
    def kv_own(u, t):
        src = (k, v)[t].at[:, columns((RING * u + y) * HEAD_DIM, HEAD_DIM)]
        dst = kv.at[u, t, pl.ds(pl.multiple_of(OWN + ROWS * y, ROWS), ROWS)]
        return pltpu.make_async_copy(src, dst, kv_recv.at[u])

    def kv_copy(u, t, j):
        there = lax.rem(y + j, RING)
        src = (k, v)[t].at[:, columns((RING * u + there) * HEAD_DIM, HEAD_DIM)]
        dst = kv.at[u, t, pl.ds(pl.multiple_of(OWN + ROWS * y, ROWS), ROWS)]
        return remote(src, dst, kv_send.at[0], kv_recv.at[u], at_y(j))

    def fix_own(t):
        return pltpu.make_async_copy((pk, pv)[t], kv.at[a, t, 0:PREFIX], fix_local.at[0])

    def fix_copy(t):
        device = (s, RING * (1 - a) + y)
        return remote(
            (pk, pv)[t], kv.at[a, t, 0:PREFIX], fix_send.at[0], fix_recv.at[0], device
        )

    def fix_share():
        ref = kv.at[1 - a, :, 0:PREFIX]
        return remote(ref, ref, fix_send.at[0], fix_recv.at[0], at_block(here + 2))

    def win_copy(u, d):
        src = kv.at[u, :, OWN:KEYS, :]
        dst = kv.at[u, :, OWN - d * BLOCK : KEYS - d * BLOCK, :]
        device = at_block(lax.rem(here + d, BLOCKS))
        return remote(src, dst, win_send.at[u], win_recv.at[u, (d - 1) // 2], device)

    def win_share(u):
        src = kv.at[u, :, OWN - 2 * BLOCK : OWN, :]
        dst = kv.at[u, :, OWN - 4 * BLOCK : OWN - 2 * BLOCK, :]
        return remote(src, dst, win_send.at[u], win_recv.at[u, 1], at_block(here + 2))

    def in_first(n, there):
        return (RING * (n // PARTS) + there) * GROUP + lax.rem(n, PARTS) * WIDE

    def in_own(n, t):
        src = (q, g)[t].at[:, columns(in_first(n, y), WIDE)]
        return pltpu.make_async_copy(src, xb.at[n, t, rows_of(y)], in_recv.at[n])

    def in_copy(n, t, j):
        src = (q, g)[t].at[:, columns(in_first(n, lax.rem(y + j, RING)), WIDE)]
        return remote(src, xb.at[n, t, rows_of(y)], in_send.at[t], in_recv.at[n], at_y(j))

    def dq_own(n):
        dst = dq.at[:, columns(in_first(n, y), WIDE)]
        return pltpu.make_async_copy(dqb.at[n, rows_of(y)], dst, dq_recv.at[0])

    def dq_copy(n, j):
        src = dqb.at[n, rows_of(lax.rem(y + j, RING))]
        dst = dq.at[:, columns(in_first(n, y), WIDE)]
        return remote(src, dst, dq_send.at[0], dq_recv.at[0], at_y(j))

    def part_copy(u, t, d):
        device = at_block(lax.rem(here + BLOCKS - d, BLOCKS))
        return remote(
            part_out.at[u, t, d - 1],
            part_in.at[u, t, d - 1],
            part_send.at[u, t],
            part_recv.at[u, t],
            device,
        )

    def merge_copy(u, t):
        device = at_block(lax.rem(here + BLOCKS - 2, BLOCKS))
        return remote(
            part_out.at[u, t, 2:4],
            merge_in.at[u, t],
            part_send.at[u, t],
            merge_recv.at[u, t],
            device,
        )

    def own_own(u, t):
        dst = (dk, dv)[t].at[:, columns((RING * u + y) * HEAD_DIM, HEAD_DIM)]
        return pltpu.make_async_copy(own_out.at[u, t, rows_of(y)], dst, own_recv.at[t])

    def own_copy(u, t, j):
        src = own_out.at[u, t, rows_of(lax.rem(y + j, RING))]
        dst = (dk, dv)[t].at[:, columns((RING * u + y) * HEAD_DIM, HEAD_DIM)]
        return remote(src, dst, own_send.at[0], own_recv.at[t], at_y(j))

    def piece_rows(r):
        return pl.ds(pl.multiple_of(PIECE * r, PIECE), PIECE)

    def pre_copy(u, i):
        r = lax.rem(s + i, SEQ)
        return remote(
            pre_out.at[u, :, piece_rows(r)],
            pre_in.at[here],
            pre_send.at[0],
            pre_recv.at[0],
            (r, RING * u + y),
        )

    def last_own(t):
        return pltpu.make_async_copy(
            pre_sum.at[t], (dpk, dpv)[t].at[piece_rows(s)], last_recv.at[t]
        )

    def last_copy(t, i):
        return remote(
            pre_sum.at[t],
            (dpk, dpv)[t].at[piece_rows(s)],
            last_send.at[0],
            last_recv.at[t],
            (lax.rem(s + i, SEQ), h),
        )

    others = range(1, RING)
    steps_back = range(1, BACK + 1)

    def send_in(n):
        for t in range(2):
            for j in (2, 1, 3):
                in_copy(n, t, j).start()

    def send_kv(u):
        for t in range(2):
            for j in (2, 1, 3):
                kv_copy(u, t, j).start()

    def send_windows(u):
        wait_for(kv.at[u, :, OWN:KEYS, :], kv_recv.at[u])
        win_copy(u, 1).start()
        win_copy(u, 2).start()

        @pl.when((place == 1) | (place == 2))
        def _():
            win_copy(u, 3).start()

        @pl.when(first_core)
        def _():
            win_copy(u, 4).start()

    def share_windows(u):
        wait_for(kv.at[u, :, OWN - 2 * BLOCK : OWN, :], win_recv.at[u, 0])

        @pl.when(first_core)
        def _():
            win_share(u).start()

    for t in range(2):
        for u in range(SLOTS):
            kv_own(u, t).start()
        fix_own(t).start()
    for n in range(STEPS):
        for t in range(2):
            in_own(n, t).start()

    for copy in small:
        copy.wait()
    @pl.when((place == 0) | (place == 3))
    def _():
        part_in[:, :, 2] = jnp.zeros((SLOTS, 2, BLOCK, HEAD_DIM), jnp.bfloat16)

    @pl.when(jnp.logical_not(first_core))
    def _():
        part_in[:, :, 3] = jnp.zeros((SLOTS, 2, BLOCK, HEAD_DIM), jnp.bfloat16)

    documents = lax.broadcasted_iota(jnp.int32, (128, 128), 0)
    limits = jnp.zeros((128, 128), jnp.int32)
    for e in range(SEGS):
        limits = jnp.where(documents == e, lens[e], limits)
    lanes = lax.broadcasted_iota(jnp.int32, (128, 128), 1)
    for i in range(PREFIX // 128):
        hidden = jnp.where(lanes + 128 * i < limits, 0.0, MASKED)
        ext[128 * i : 128 * (i + 1), :] = hidden.T.astype(jnp.bfloat16)
    for i in range(WINDOW // 128):
        row = 2 * here - 2 * BACK + i
        names = jnp.broadcast_to(seg[pl.ds(jnp.maximum(row, 0), 1), :], (128, 128))
        real = jnp.full((128, 128), row, jnp.int32) >= 0
        hidden = jnp.where((names == documents) & real, 0.0, MASKED)
        ext[PREFIX + 128 * i : PREFIX + 128 * (i + 1), :] = hidden.T.astype(jnp.bfloat16)
        if i >= 2 * BACK:
            picked = jnp.where(names == documents, 1.0, 0.0)
            first = 128 * (i - 2 * BACK)
            qx[first : first + 128, :] = picked.T.astype(jnp.bfloat16)

    pl.semaphore_wait(barrier, RING - 1 + BLOCKS - 1)
    send_kv(0)
    @pl.when(first_core)
    def _():
        for t in range(2):
            fix_copy(t).start()

    send_in(0)
    send_kv(1)

    send_windows(0)
    for n in range(1, STEPS):
        send_in(n)

    def prepare(u):
        wait_for(kv.at[u, :, PREFIX : OWN - 2 * BLOCK, :], win_recv.at[u, 1])
        for i in range(KEYS // 128):
            part = kv[u, 0, 128 * i : 128 * (i + 1), :].astype(jnp.float32)
            kt[:, 128 * i : 128 * (i + 1)] = part.T.astype(jnp.bfloat16)
        acc[...] = jnp.zeros_like(acc)

    passes = ((s_0, d_0, p_0, ds_0), (s_1, d_1, p_1, ds_1))

    def key_rows(i, cut):
        first, size = cut
        return pl.ds(first if first < PREFIX else first + SUB * i, size)

    def load_rows(n, t, i):
        rows = pl.ds(SUB * i, SUB)
        return jnp.concatenate(
            [xb[n, t, rows, HEAD_DIM * x : HEAD_DIM * (x + 1)] for x in range(HEADS)], axis=0
        )

    def score(u, i, q2, g2):
        s_ref, d_ref, _, _ = passes[i]
        marks = jnp.concatenate([qx[pl.ds(SUB * i, SUB), :]] * HEADS, axis=0)
        q_wide = jnp.concatenate([q2, marks], axis=1)

        def keys(cut):
            rows = key_rows(i, cut)
            wide = jnp.concatenate([kv[u, 0, rows, :], ext[rows, :]], axis=1)
            s_ref[pl.ds(*cut), :] = dot_nt(wide, q_wide)

        def values(cut):
            d_ref[pl.ds(*cut), :] = dot_nt(kv[u, 1, key_rows(i, cut), :], g2)

        for cut in CUTS:
            yield lambda: keys(cut)
        for cut in CUTS:
            yield lambda: values(cut)

    def weigh(i, first):
        s_ref, d_ref, p_ref, ds_ref = passes[i]
        tiles = [pl.ds(f, TILE) for f in range(0, SPAN, TILE)]
        key_at = lax.broadcasted_iota(jnp.int32, (SUB, HALF), 0)
        row_at = lax.rem(lax.broadcasted_iota(jnp.int32, (SUB, HALF), 1), SUB)

        def fold(tile):
            return tile.reshape(TILE // 8, 8, HALF)

        for c in range(0, WIDE, HALF):
            cols = pl.ds(c, HALF)
            out = pl.ds(pl.multiple_of(first + c, HALF), HALF)
            has = {}

            def begin():
                last = pl.ds(SPAN - SUB, SUB)
                s_ref[last, cols] = jnp.where(key_at <= row_at, s_ref[last, cols], MASKED)
                has["peak"] = jnp.full((8, HALF), MASKED, jnp.float32)
                has["total"] = jnp.zeros((8, HALF), jnp.float32)
                has["weighted"] = jnp.zeros((8, HALF), jnp.float32)

            def top(tile):
                has["peak"] = jnp.maximum(has["peak"], jnp.max(fold(s_ref[tile, cols]), axis=0))

            def level():
                has["peak"] = jnp.max(has["peak"], axis=0, keepdims=True)

            def weight(tile):
                weights = jnp.exp2((s_ref[tile, cols] - has["peak"]) * EXP_SCALE)
                s_ref[tile, cols] = weights
                has["total"] += jnp.sum(fold(weights), axis=0)
                has["weighted"] += jnp.sum(fold(weights * d_ref[tile, cols]), axis=0)

            def settle():
                has["inverse"] = 1.0 / jnp.sum(has["total"], axis=0, keepdims=True)
                weighted = jnp.sum(has["weighted"], axis=0, keepdims=True)
                has["delta"] = weighted * has["inverse"]

            def grade(tile):
                probs = s_ref[tile, cols] * has["inverse"]
                p_ref[tile, cols] = probs.astype(jnp.bfloat16)
                score_grad = probs * (d_ref[tile, cols] - has["delta"])
                ds_ref[tile, out] = score_grad.astype(jnp.bfloat16)

            yield begin
            for tile in tiles:
                yield lambda: top(tile)
            yield level
            for tile in tiles:
                yield lambda: weight(tile)
            yield settle
            for tile in tiles:
                yield lambda: grade(tile)

    def gather_up(i, first, q2, g2):
        _, _, p_ref, ds_ref = passes[i]
        cols = pl.ds(pl.multiple_of(first, WIDE), WIDE)

        def values(cut):
            acc[1, key_rows(i, cut), :] += dot_nn(p_ref[pl.ds(*cut), :], g2)

        def keys(cut):
            acc[0, key_rows(i, cut), :] += dot_nn(ds_ref[pl.ds(*cut), cols], q2)

        for cut in CUTS:
            yield lambda: values(cut)
        for cut in CUTS:
            yield lambda: keys(cut)

    def together(products, count, others, other_count):
        done = 0
        for i in range(other_count):
            while done < count and done * other_count <= i * count:
                next(products)()
                done += 1
            next(others)()
        for rest in products:
            rest()

    def attend(n, u):
        first = lax.rem(n, PARTS) * WIDE
        held = [[load_rows(n, t, i) for t in range(2)] for i in range(2)]
        products = 2 * len(CUTS)
        passing = WIDE // HALF * (3 * (SPAN // TILE) + 3)
        for do in score(u, 0, *held[0]):
            do()
        together(score(u, 1, *held[1]), products, weigh(0, first), passing)
        together(gather_up(0, first, *held[0]), products, weigh(1, first), passing)
        for do in gather_up(1, first, *held[1]):
            do()

    def query_part(u, between=None):
        for i in range(2):
            if i == 1 and between is not None:
                between(u)
            _, _, _, ds_ref = passes[i]
            rows = pl.ds(SUB * i, SUB)
            near = pl.ds(PREFIX + SUB * i, NEAR)
            grad = dot_nn(kt[:, 0:PREFIX], ds_ref[0:PREFIX, :])
            grad += dot_nn(kt[:, near], ds_ref[PREFIX:SPAN, :])
            grad = (grad * SCALE).T.astype(jnp.bfloat16)
            for x in range(PARTS * HEADS):
                cols = pl.ds(HEAD_DIM * (x % HEADS), HEAD_DIM)
                dqb[PARTS * u + x // HEADS, rows, cols] = grad[SUB * x : SUB * (x + 1)]
        for n in range(PARTS):
            for j in (2, 1, 3):
                dq_copy(PARTS * u + n, j).start()
            dq_own(PARTS * u + n).start()

    def close(u):
        for t in (1, 0):
            for d in (3, 4, 1, 2):
                low = OWN - d * BLOCK
                part_out[u, t, d - 1] = acc[t, low : low + BLOCK, :].astype(jnp.bfloat16)

            @pl.when(first_core)
            def _():
                part_copy(u, t, 3).start()
                part_copy(u, t, 4).start()

            @pl.when(jnp.logical_not(first_core))
            def _():
                merge_copy(u, t).start()
                part_copy(u, t, 1).start()
                part_copy(u, t, 2).start()

        for t in range(2):
            pre_out[u, t] = acc[t, 0:PREFIX, :].astype(jnp.bfloat16)
            own_sum[u, t] = acc[t, OWN:KEYS, :]

        @pl.when(a == u)
        def _():
            pre_in[here] = pre_out[u, :, piece_rows(s), :]

        @pl.when(a != u)
        def _():
            pre_copy(u, 0).start()

        def spread(i, carry):
            pre_copy(u, i).start()
            return carry

        lax.fori_loop(1, SEQ, spread, 0)

    def merge(u):
        @pl.when(first_core)
        def _():
            for t in (1, 0):
                wait_for(merge_in.at[u, t], merge_recv.at[u, t])
                for d in (1, 2):
                    both = part_out[u, t, d - 1].astype(jnp.float32)
                    both += merge_in[u, t, d - 1].astype(jnp.float32)
                    part_out[u, t, d - 1] = both.astype(jnp.bfloat16)
                    part_copy(u, t, d).start()

    def finish(u):
        for t in (1, 0):
            for at, count in enumerate((3, 4, 3, 2)):

                @pl.when(place == at)
                def _():
                    wait_for(part_in.at[u, t, 0:count], part_recv.at[u, t])

            whole = own_sum[u, t]
            for d in steps_back:
                whole += part_in[u, t, d - 1].astype(jnp.float32)
            if t == 0:
                whole = whole * SCALE
            own_out[u, t] = whole.astype(jnp.bfloat16)
            for j in (2, 1, 3):
                own_copy(u, t, j).start()
            own_own(u, t).start()

    def hand_prefix(u):
        @pl.when(a == u)
        def _():
            wait_for(pre_in.at[0 : BLOCKS - 1], pre_recv.at[0])
            for t in range(2):
                whole = jnp.sum(pre_in[:, t].astype(jnp.float32), axis=0)
                if t == 0:
                    whole = whole * SCALE
                pre_sum[t] = whole.astype(jnp.bfloat16)
            for t in range(2):
                for i in range(1, SEQ):
                    last_copy(t, i).start()
                last_own(t).start()

    wait_for(kv.at[0, :, 0:PREFIX], fix_local.at[0])
    wait_for(kv.at[0, :, 0:PREFIX], fix_recv.at[0])

    @pl.when(first_core)
    def _():
        fix_share().start()


    def step(n, carry):
        u = n // PARTS

        @pl.when(n == 0)
        def _():
            share_windows(0)
            send_windows(1)

        @pl.when(lax.rem(n, PARTS) == 0)
        def _():
            prepare(u)

        wait_for(xb.at[n], in_recv.at[n])

        attend(n, u)

        @pl.when(n == PARTS - 1)
        def _():
            share_windows(1)

        @pl.when(lax.rem(n, PARTS) == PARTS - 1)
        def _():
            close(u)

        @pl.when(n == PARTS - 1)
        def _():
            query_part(0)

        @pl.when(n == PARTS - 1)
        def _():
            merge(0)

        @pl.when(n == PARTS)
        def _():
            finish(0)
            hand_prefix(0)

        return carry

    lax.fori_loop(0, STEPS, step, 0)

    query_part(1, merge)
    hand_prefix(1)
    finish(1)

    for t in range(2):
        wait_for(xb.at[0:3, t], in_send.at[t])
        wait_for((dk, dv)[t], own_recv.at[t])
        wait_for((dpk, dpv)[t], last_recv.at[t])
    wait_for(dqb.at[0:3], dq_send.at[0])
    wait_for(dq, dq_recv.at[0])
    wait_for(own_out.at[:, :, 0 : BLOCK - ROWS], kv_send.at[0])
    wait_for(own_out.at[:, :, 0 : BLOCK - ROWS], own_send.at[0])
    @pl.when(first_core)
    def _():
        wait_for(pre_out, fix_send.at[0])

    wait_for(pre_out.at[0, :, 0 : PREFIX - PIECE], last_send.at[0])
    wait_for(pre_in.at[0 : BLOCKS - 1], pre_send.at[0])
    for u in range(SLOTS):
        for at, sent in enumerate((5, 6, 3, 2)):

            @pl.when(place == at)
            def _():
                wait_for(kv.at[u, :, 0 : sent * BLOCK, :], win_send.at[u])

        for t in range(2):
            wait_for(part_out.at[u, t], part_send.at[u, t])


def hand_over(*refs):
    count = (len(refs) - 2) // 3
    before, after, held = refs[:count], refs[count : 2 * count], refs[2 * count : 3 * count]
    arrived, stored = refs[-2:]
    pieces = []
    for i in range(count):
        rows = before[i].shape[0]
        size = 16 if before[i].shape[1] > GROUP else rows
        for first in range(0, rows, size):
            n = len(pieces)
            part = pl.ds(first, size)
            pieces.append(
                (
                    pltpu.make_async_copy(before[i].at[part], held[i].at[part], arrived.at[n]),
                    pltpu.make_async_copy(held[i].at[part], after[i].at[part], stored.at[n]),
                )
            )
    for load, store in pieces:
        load.start()
    for load, store in pieces:
        load.wait()
        store.start()
    for load, store in pieces:
        store.wait()


def on_device(queries, keys, values, out_grad, prefix_keys, prefix_values, seg_ids, prefix_lens):
    bf16, f32 = jnp.bfloat16, jnp.float32
    dma = pltpu.SemaphoreType.DMA
    hbm = pl.BlockSpec(memory_space=pl.ANY)
    arrays = [
        ((STEPS, 2, BLOCK, WIDE), bf16),
        ((SLOTS, 2, KEYS, HEAD_DIM), bf16),
        ((KEYS, 128), bf16),
        ((BLOCK, 128), bf16),
        ((HEAD_DIM, KEYS), bf16),
        ((2, KEYS, HEAD_DIM), f32),
        ((SLOTS, 2, BLOCK, HEAD_DIM), f32),
        ((SPAN, WIDE), f32),
        ((SPAN, WIDE), f32),
        ((SPAN, WIDE), bf16),
        ((SPAN, GROUP), bf16),
        ((SPAN, WIDE), f32),
        ((SPAN, WIDE), f32),
        ((SPAN, WIDE), bf16),
        ((SPAN, GROUP), bf16),
        ((STEPS, BLOCK, WIDE), bf16),
        ((SLOTS, 2, BACK, BLOCK, HEAD_DIM), bf16),
        ((SLOTS, 2, BACK, BLOCK, HEAD_DIM), bf16),
        ((SLOTS, 2, 2, BLOCK, HEAD_DIM), bf16),
        ((SLOTS, 2, BLOCK, HEAD_DIM), bf16),
        ((SLOTS, 2, PREFIX, HEAD_DIM), bf16),
        ((BLOCKS, 2, PIECE, HEAD_DIM), bf16),
        ((2, PIECE, HEAD_DIM), bf16),
    ]
    semaphores = [
        2,
        1,
        SLOTS,
        1,
        1,
        1,
        SLOTS,
        (SLOTS, 2),
        2,
        STEPS,
        1,
        1,
        (SLOTS, 2),
        (SLOTS, 2),
        (SLOTS, 2),
        1,
        2,
        1,
        1,
        1,
        2,
    ]
    results = (
        jax.ShapeDtypeStruct(queries.shape, bf16),
        jax.ShapeDtypeStruct(keys.shape, bf16),
        jax.ShapeDtypeStruct(values.shape, bf16),
        jax.ShapeDtypeStruct(prefix_keys.shape, bf16),
        jax.ShapeDtypeStruct(prefix_values.shape, bf16),
    )
    raw = pl.pallas_call(
        kernel,
        out_shape=results,
        in_specs=[hbm] * 8,
        out_specs=(hbm,) * 5,
        scratch_shapes=[pltpu.VMEM(shape, kind) for shape, kind in arrays]
        + [pltpu.VMEM((64, 128), jnp.int32), pltpu.SMEM((SEGS,), jnp.int32)]
        + [dma(size if isinstance(size, tuple) else (size,)) for size in semaphores],
        compiler_params=pltpu.CompilerParams(
            collective_id=0, has_side_effects=True, vmem_limit_bytes=56 * 1024 * 1024
        ),
        cost_estimate=pl.CostEstimate(
            flops=4096 * SPAN * HEAD_DIM * 10,
            bytes_accessed=4 * 1024 * 1024,
            transcendentals=4096 * SPAN,
        ),
    )(
        queries,
        out_grad,
        keys,
        values,
        prefix_keys,
        prefix_values,
        seg_ids.reshape(64, 128),
        prefix_lens,
    )
    return pl.pallas_call(
        hand_over,
        out_shape=results,
        in_specs=[hbm] * len(results),
        out_specs=(hbm,) * len(results),
        scratch_shapes=[pltpu.VMEM(x.shape, x.dtype) for x in results] + [dma((16,)), dma((16,))],
    )(*raw)


def solution(mesh):
    return jax.shard_map(
        on_device,
        mesh=mesh,
        in_specs=(
            P(("seq", "head"), None),
            P(("seq", "head"), None),
            P(("seq", "head"), None),
            P(("seq", "head"), None),
            P(None, "head"),
            P(None, "head"),
            P(),
            P(),
        ),
        out_specs=(
            P(("seq", "head"), None),
            P(("seq", "head"), None),
            P(("seq", "head"), None),
            P(None, "head"),
            P(None, "head"),
        ),
        check_vma=False,
    )
```

```python
import math

import jax
import jax.numpy as jnp
from jax import lax
from jax.experimental import pallas as pl
from jax.experimental.pallas import tpu as pltpu
from jax.sharding import PartitionSpec as P

MESH = pl.DeviceIdType.MESH

HEAD_DIM = 128
PREFIX = 256
RING = 4
ROWS = 64
BLOCK = RING * ROWS
BACK = 4
WINDOW = (BACK + 1) * BLOCK
KEYS = PREFIX + WINDOW
OWN = PREFIX + BACK * BLOCK
SLOTS = 2
HEADS = 4
PARTS = 2
STEPS = SLOTS * PARTS
WIDE = HEADS * HEAD_DIM
GROUP = PARTS * WIDE
SUB = 128
NEAR = 1024 + SUB
SPAN = PREFIX + NEAR
TILE = 128
HALF = 256
CUTS = [(0, PREFIX)] + [(PREFIX + NEAR // 3 * i, NEAR // 3) for i in range(3)]
BLOCKS = 32
SEQ = 16
SEGS = 32
SCALE = HEAD_DIM**-0.5
EXP_SCALE = SCALE / math.log(2.0)
MASKED = -1e30
PIECE = PREFIX // SEQ


def dot_nt(a, b):
    return lax.dot_general(a, b, (((1,), (1,)), ((), ())), preferred_element_type=jnp.float32)


def dot_nn(a, b):
    return lax.dot_general(a, b, (((1,), (0,)), ((), ())), preferred_element_type=jnp.float32)


def kernel(
    q,
    g,
    k,
    v,
    pk,
    pv,
    seg_hbm,
    lens_hbm,
    dq,
    dk,
    dv,
    dpk,
    dpv,
    xb,
    kv,
    ext,
    qx,
    kt,
    acc,
    own_sum,
    s_0,
    d_0,
    p_0,
    ds_0,
    s_1,
    d_1,
    p_1,
    ds_1,
    dqb,
    part_out,
    part_in,
    merge_in,
    own_out,
    pre_out,
    pre_in,
    pre_sum,
    seg,
    lens,
    small_sem,
    kv_send,
    kv_recv,
    fix_local,
    fix_send,
    fix_recv,
    win_send,
    win_recv,
    in_send,
    in_recv,
    dq_send,
    dq_recv,
    part_send,
    part_recv,
    merge_recv,
    own_send,
    own_recv,
    pre_send,
    pre_recv,
    last_send,
    last_recv,
):
    s = lax.axis_index("seq")
    h = lax.axis_index("head")
    y = lax.rem(h, RING)
    a = h // RING
    here = 2 * s + a
    place = lax.rem(here, 4)
    first_core = place < 2

    def at_y(j):
        return (s, RING * a + lax.rem(y + j, RING))

    def at_block(b):
        return (b // 2, lax.rem(b, 2) * RING + y)

    def columns(first, size):
        return pl.ds(pl.multiple_of(first, 128), size)

    def rows_of(j):
        return pl.ds(pl.multiple_of(ROWS * j, ROWS), ROWS)

    def remote(src, dst, send, recv, device):
        return pltpu.make_async_remote_copy(
            src_ref=src,
            dst_ref=dst,
            send_sem=send,
            recv_sem=recv,
            device_id=device,
            device_id_type=MESH,
        )

    small = [
        pltpu.make_async_copy(seg_hbm, seg, small_sem.at[0]),
        pltpu.make_async_copy(lens_hbm, lens, small_sem.at[1]),
    ]
    for copy in small:
        copy.start()

    def wait_for(ref, sem):
        pltpu.make_async_copy(ref, ref, sem).wait()

    barrier = pltpu.get_barrier_semaphore()
    for j in range(1, RING):
        pl.semaphore_signal(barrier, inc=1, device_id=at_y(j), device_id_type=MESH)

    def greet(d, carry):
        there = at_block(lax.rem(here + d, BLOCKS))
        pl.semaphore_signal(barrier, inc=1, device_id=there, device_id_type=MESH)
        return carry

    lax.fori_loop(1, BLOCKS, greet, 0)
    def kv_own(u, t):
        src = (k, v)[t].at[:, columns((RING * u + y) * HEAD_DIM, HEAD_DIM)]
        dst = kv.at[u, t, pl.ds(pl.multiple_of(OWN + ROWS * y, ROWS), ROWS)]
        return pltpu.make_async_copy(src, dst, kv_recv.at[u])

    def kv_copy(u, t, j):
        there = lax.rem(y + j, RING)
        src = (k, v)[t].at[:, columns((RING * u + there) * HEAD_DIM, HEAD_DIM)]
        dst = kv.at[u, t, pl.ds(pl.multiple_of(OWN + ROWS * y, ROWS), ROWS)]
        return remote(src, dst, kv_send.at[0], kv_recv.at[u], at_y(j))

    def fix_own(t):
        return pltpu.make_async_copy((pk, pv)[t], kv.at[a, t, 0:PREFIX], fix_local.at[0])

    def fix_copy(t):
        device = (s, RING * (1 - a) + y)
        return remote(
            (pk, pv)[t], kv.at[a, t, 0:PREFIX], fix_send.at[0], fix_recv.at[0], device
        )

    def fix_share():
        ref = kv.at[1 - a, :, 0:PREFIX]
        return remote(ref, ref, fix_send.at[0], fix_recv.at[0], at_block(here + 2))

    def win_copy(u, d):
        src = kv.at[u, :, OWN:KEYS, :]
        dst = kv.at[u, :, OWN - d * BLOCK : KEYS - d * BLOCK, :]
        device = at_block(lax.rem(here + d, BLOCKS))
        return remote(src, dst, win_send.at[u], win_recv.at[u, (d - 1) // 2], device)

    def win_share(u):
        src = kv.at[u, :, OWN - 2 * BLOCK : OWN, :]
        dst = kv.at[u, :, OWN - 4 * BLOCK : OWN - 2 * BLOCK, :]
        return remote(src, dst, win_send.at[u], win_recv.at[u, 1], at_block(here + 2))

    def in_first(n, there):
        return (RING * (n // PARTS) + there) * GROUP + lax.rem(n, PARTS) * WIDE

    def in_own(n, t):
        src = (q, g)[t].at[:, columns(in_first(n, y), WIDE)]
        return pltpu.make_async_copy(src, xb.at[n, t, rows_of(y)], in_recv.at[n])

    def in_copy(n, t, j):
        src = (q, g)[t].at[:, columns(in_first(n, lax.rem(y + j, RING)), WIDE)]
        return remote(src, xb.at[n, t, rows_of(y)], in_send.at[t], in_recv.at[n], at_y(j))

    def dq_own(n):
        dst = dq.at[:, columns(in_first(n, y), WIDE)]
        return pltpu.make_async_copy(dqb.at[n, rows_of(y)], dst, dq_recv.at[0])

    def dq_copy(n, j):
        src = dqb.at[n, rows_of(lax.rem(y + j, RING))]
        dst = dq.at[:, columns(in_first(n, y), WIDE)]
        return remote(src, dst, dq_send.at[0], dq_recv.at[0], at_y(j))

    def part_copy(u, t, d):
        device = at_block(lax.rem(here + BLOCKS - d, BLOCKS))
        return remote(
            part_out.at[u, t, d - 1],
            part_in.at[u, t, d - 1],
            part_send.at[u, t],
            part_recv.at[u, t],
            device,
        )

    def merge_copy(u, t):
        device = at_block(lax.rem(here + BLOCKS - 2, BLOCKS))
        return remote(
            part_out.at[u, t, 2:4],
            merge_in.at[u, t],
            part_send.at[u, t],
            merge_recv.at[u, t],
            device,
        )

    def own_own(u, t):
        dst = (dk, dv)[t].at[:, columns((RING * u + y) * HEAD_DIM, HEAD_DIM)]
        return pltpu.make_async_copy(own_out.at[u, t, rows_of(y)], dst, own_recv.at[t])

    def own_copy(u, t, j):
        src = own_out.at[u, t, rows_of(lax.rem(y + j, RING))]
        dst = (dk, dv)[t].at[:, columns((RING * u + y) * HEAD_DIM, HEAD_DIM)]
        return remote(src, dst, own_send.at[0], own_recv.at[t], at_y(j))

    def piece_rows(r):
        return pl.ds(pl.multiple_of(PIECE * r, PIECE), PIECE)

    def pre_copy(u, i):
        r = lax.rem(s + i, SEQ)
        return remote(
            pre_out.at[u, :, piece_rows(r)],
            pre_in.at[here],
            pre_send.at[0],
            pre_recv.at[0],
            (r, RING * u + y),
        )

    def last_own(t):
        return pltpu.make_async_copy(
            pre_sum.at[t], (dpk, dpv)[t].at[piece_rows(s)], last_recv.at[t]
        )

    def last_copy(t, i):
        return remote(
            pre_sum.at[t],
            (dpk, dpv)[t].at[piece_rows(s)],
            last_send.at[0],
            last_recv.at[t],
            (lax.rem(s + i, SEQ), h),
        )

    others = range(1, RING)
    steps_back = range(1, BACK + 1)

    def send_in(n):
        for t in range(2):
            for j in (2, 1, 3):
                in_copy(n, t, j).start()

    def send_kv(u):
        for t in range(2):
            for j in (2, 1, 3):
                kv_copy(u, t, j).start()

    def send_windows(u):
        wait_for(kv.at[u, :, OWN:KEYS, :], kv_recv.at[u])
        win_copy(u, 1).start()
        win_copy(u, 2).start()

        @pl.when((place == 1) | (place == 2))
        def _():
            win_copy(u, 3).start()

        @pl.when(first_core)
        def _():
            win_copy(u, 4).start()

    def share_windows(u):
        wait_for(kv.at[u, :, OWN - 2 * BLOCK : OWN, :], win_recv.at[u, 0])

        @pl.when(first_core)
        def _():
            win_share(u).start()

    for t in range(2):
        for u in range(SLOTS):
            kv_own(u, t).start()
        fix_own(t).start()
    for n in range(STEPS):
        for t in range(2):
            in_own(n, t).start()

    for copy in small:
        copy.wait()
    @pl.when((place == 0) | (place == 3))
    def _():
        part_in[:, :, 2] = jnp.zeros((SLOTS, 2, BLOCK, HEAD_DIM), jnp.bfloat16)

    @pl.when(jnp.logical_not(first_core))
    def _():
        part_in[:, :, 3] = jnp.zeros((SLOTS, 2, BLOCK, HEAD_DIM), jnp.bfloat16)

    documents = lax.broadcasted_iota(jnp.int32, (128, 128), 0)
    limits = jnp.zeros((128, 128), jnp.int32)
    for e in range(SEGS):
        limits = jnp.where(documents == e, lens[e], limits)
    lanes = lax.broadcasted_iota(jnp.int32, (128, 128), 1)
    for i in range(PREFIX // 128):
        hidden = jnp.where(lanes + 128 * i < limits, 0.0, MASKED)
        ext[128 * i : 128 * (i + 1), :] = hidden.T.astype(jnp.bfloat16)
    for i in range(WINDOW // 128):
        row = 2 * here - 2 * BACK + i
        names = jnp.broadcast_to(seg[pl.ds(jnp.maximum(row, 0), 1), :], (128, 128))
        real = jnp.full((128, 128), row, jnp.int32) >= 0
        hidden = jnp.where((names == documents) & real, 0.0, MASKED)
        ext[PREFIX + 128 * i : PREFIX + 128 * (i + 1), :] = hidden.T.astype(jnp.bfloat16)
        if i >= 2 * BACK:
            picked = jnp.where(names == documents, 1.0, 0.0)
            first = 128 * (i - 2 * BACK)
            qx[first : first + 128, :] = picked.T.astype(jnp.bfloat16)

    pl.semaphore_wait(barrier, RING - 1 + BLOCKS - 1)
    send_kv(0)
    @pl.when(first_core)
    def _():
        for t in range(2):
            fix_copy(t).start()

    send_in(0)
    send_kv(1)

    send_windows(0)
    for n in range(1, STEPS):
        send_in(n)

    def prepare(u):
        wait_for(kv.at[u, :, PREFIX : OWN - 2 * BLOCK, :], win_recv.at[u, 1])
        for i in range(KEYS // 128):
            part = kv[u, 0, 128 * i : 128 * (i + 1), :].astype(jnp.float32)
            kt[:, 128 * i : 128 * (i + 1)] = part.T.astype(jnp.bfloat16)
        acc[...] = jnp.zeros_like(acc)

    passes = ((s_0, d_0, p_0, ds_0), (s_1, d_1, p_1, ds_1))

    def key_rows(i, cut):
        first, size = cut
        return pl.ds(first if first < PREFIX else first + SUB * i, size)

    def load_rows(n, t, i):
        rows = pl.ds(SUB * i, SUB)
        return jnp.concatenate(
            [xb[n, t, rows, HEAD_DIM * x : HEAD_DIM * (x + 1)] for x in range(HEADS)], axis=0
        )

    def score(u, i, q2, g2):
        s_ref, d_ref, _, _ = passes[i]
        marks = jnp.concatenate([qx[pl.ds(SUB * i, SUB), :]] * HEADS, axis=0)
        q_wide = jnp.concatenate([q2, marks], axis=1)

        def keys(cut):
            rows = key_rows(i, cut)
            wide = jnp.concatenate([kv[u, 0, rows, :], ext[rows, :]], axis=1)
            s_ref[pl.ds(*cut), :] = dot_nt(wide, q_wide)

        def values(cut):
            d_ref[pl.ds(*cut), :] = dot_nt(kv[u, 1, key_rows(i, cut), :], g2)

        for cut in CUTS:
            yield lambda: keys(cut)
        for cut in CUTS:
            yield lambda: values(cut)

    def weigh(i, first):
        s_ref, d_ref, p_ref, ds_ref = passes[i]
        tiles = [pl.ds(f, TILE) for f in range(0, SPAN, TILE)]
        key_at = lax.broadcasted_iota(jnp.int32, (SUB, HALF), 0)
        row_at = lax.rem(lax.broadcasted_iota(jnp.int32, (SUB, HALF), 1), SUB)

        def fold(tile):
            return tile.reshape(TILE // 8, 8, HALF)

        for c in range(0, WIDE, HALF):
            cols = pl.ds(c, HALF)
            out = pl.ds(pl.multiple_of(first + c, HALF), HALF)
            has = {}

            def begin():
                last = pl.ds(SPAN - SUB, SUB)
                s_ref[last, cols] = jnp.where(key_at <= row_at, s_ref[last, cols], MASKED)
                has["peak"] = jnp.full((8, HALF), MASKED, jnp.float32)
                has["total"] = jnp.zeros((8, HALF), jnp.float32)
                has["weighted"] = jnp.zeros((8, HALF), jnp.float32)

            def top(tile):
                has["peak"] = jnp.maximum(has["peak"], jnp.max(fold(s_ref[tile, cols]), axis=0))

            def level():
                has["peak"] = jnp.max(has["peak"], axis=0, keepdims=True)

            def weight(tile):
                weights = jnp.exp2((s_ref[tile, cols] - has["peak"]) * EXP_SCALE)
                s_ref[tile, cols] = weights
                has["total"] += jnp.sum(fold(weights), axis=0)
                has["weighted"] += jnp.sum(fold(weights * d_ref[tile, cols]), axis=0)

            def settle():
                has["inverse"] = 1.0 / jnp.sum(has["total"], axis=0, keepdims=True)
                weighted = jnp.sum(has["weighted"], axis=0, keepdims=True)
                has["delta"] = weighted * has["inverse"]

            def grade(tile):
                probs = s_ref[tile, cols] * has["inverse"]
                p_ref[tile, cols] = probs.astype(jnp.bfloat16)
                score_grad = probs * (d_ref[tile, cols] - has["delta"])
                ds_ref[tile, out] = score_grad.astype(jnp.bfloat16)

            yield begin
            for tile in tiles:
                yield lambda: top(tile)
            yield level
            for tile in tiles:
                yield lambda: weight(tile)
            yield settle
            for tile in tiles:
                yield lambda: grade(tile)

    def gather_up(i, first, q2, g2):
        _, _, p_ref, ds_ref = passes[i]
        cols = pl.ds(pl.multiple_of(first, WIDE), WIDE)

        def values(cut):
            acc[1, key_rows(i, cut), :] += dot_nn(p_ref[pl.ds(*cut), :], g2)

        def keys(cut):
            acc[0, key_rows(i, cut), :] += dot_nn(ds_ref[pl.ds(*cut), cols], q2)

        for cut in CUTS:
            yield lambda: values(cut)
        for cut in CUTS:
            yield lambda: keys(cut)

    def together(products, count, others, other_count):
        done = 0
        for i in range(other_count):
            while done < count and done * other_count <= i * count:
                next(products)()
                done += 1
            next(others)()
        for rest in products:
            rest()

    def attend(n, u):
        first = lax.rem(n, PARTS) * WIDE
        held = [[load_rows(n, t, i) for t in range(2)] for i in range(2)]
        products = 2 * len(CUTS)
        passing = WIDE // HALF * (3 * (SPAN // TILE) + 3)
        for do in score(u, 0, *held[0]):
            do()
        together(score(u, 1, *held[1]), products, weigh(0, first), passing)
        together(gather_up(0, first, *held[0]), products, weigh(1, first), passing)
        for do in gather_up(1, first, *held[1]):
            do()

    def query_part(u, between=None):
        for i in range(2):
            if i == 1 and between is not None:
                between(u)
            _, _, _, ds_ref = passes[i]
            rows = pl.ds(SUB * i, SUB)
            near = pl.ds(PREFIX + SUB * i, NEAR)
            grad = dot_nn(kt[:, 0:PREFIX], ds_ref[0:PREFIX, :])
            grad += dot_nn(kt[:, near], ds_ref[PREFIX:SPAN, :])
            grad = (grad * SCALE).T.astype(jnp.bfloat16)
            for x in range(PARTS * HEADS):
                cols = pl.ds(HEAD_DIM * (x % HEADS), HEAD_DIM)
                dqb[PARTS * u + x // HEADS, rows, cols] = grad[SUB * x : SUB * (x + 1)]
        for n in range(PARTS):
            for j in (2, 1, 3):
                dq_copy(PARTS * u + n, j).start()
            dq_own(PARTS * u + n).start()

    def close(u):
        for t in range(2):
            pre_out[u, t] = acc[t, 0:PREFIX, :].astype(jnp.bfloat16)

        @pl.when(a == u)
        def _():
            pre_in[here] = pre_out[u, :, piece_rows(s), :]

        @pl.when(a != u)
        def _():
            pre_copy(u, 0).start()

        def spread(i, carry):
            pre_copy(u, i).start()
            return carry

        lax.fori_loop(1, SEQ, spread, 0)

        for t in (1, 0):
            for d in (3, 4, 1, 2):
                low = OWN - d * BLOCK
                part_out[u, t, d - 1] = acc[t, low : low + BLOCK, :].astype(jnp.bfloat16)

            @pl.when(first_core)
            def _():
                part_copy(u, t, 3).start()
                part_copy(u, t, 4).start()

            @pl.when(jnp.logical_not(first_core))
            def _():
                merge_copy(u, t).start()
                part_copy(u, t, 1).start()
                part_copy(u, t, 2).start()

        for t in range(2):
            own_sum[u, t] = acc[t, OWN:KEYS, :]


    def merge(u):
        @pl.when(first_core)
        def _():
            for t in (1, 0):
                wait_for(merge_in.at[u, t], merge_recv.at[u, t])
                for d in (1, 2):
                    both = part_out[u, t, d - 1].astype(jnp.float32)
                    both += merge_in[u, t, d - 1].astype(jnp.float32)
                    part_out[u, t, d - 1] = both.astype(jnp.bfloat16)
                    part_copy(u, t, d).start()

    def finish(u):
        for t in (1, 0):
            for at, count in enumerate((3, 4, 3, 2)):

                @pl.when(place == at)
                def _():
                    wait_for(part_in.at[u, t, 0:count], part_recv.at[u, t])

            whole = own_sum[u, t]
            for d in steps_back:
                whole += part_in[u, t, d - 1].astype(jnp.float32)
            if t == 0:
                whole = whole * SCALE
            own_out[u, t] = whole.astype(jnp.bfloat16)
            for j in (2, 1, 3):
                own_copy(u, t, j).start()
            own_own(u, t).start()

    def hand_prefix(u):
        @pl.when(a == u)
        def _():
            wait_for(pre_in.at[0 : BLOCKS - 1], pre_recv.at[0])
            for t in range(2):
                whole = jnp.sum(pre_in[:, t].astype(jnp.float32), axis=0)
                if t == 0:
                    whole = whole * SCALE
                pre_sum[t] = whole.astype(jnp.bfloat16)
            for t in range(2):
                for i in range(1, SEQ):
                    last_copy(t, i).start()
                last_own(t).start()

    wait_for(kv.at[0, :, 0:PREFIX], fix_local.at[0])
    wait_for(kv.at[0, :, 0:PREFIX], fix_recv.at[0])

    @pl.when(first_core)
    def _():
        fix_share().start()


    def step(n, carry):
        u = n // PARTS

        @pl.when(n == 0)
        def _():
            share_windows(0)
            send_windows(1)

        @pl.when(lax.rem(n, PARTS) == 0)
        def _():
            prepare(u)

        wait_for(xb.at[n], in_recv.at[n])

        attend(n, u)

        @pl.when(n == PARTS - 1)
        def _():
            share_windows(1)

        @pl.when(lax.rem(n, PARTS) == PARTS - 1)
        def _():
            close(u)

        @pl.when(n == PARTS - 1)
        def _():
            query_part(0)

        @pl.when(n == PARTS - 1)
        def _():
            merge(0)

        @pl.when(n == PARTS)
        def _():
            finish(0)
            hand_prefix(0)

        return carry

    lax.fori_loop(0, STEPS, step, 0)

    query_part(1, merge)
    hand_prefix(1)
    finish(1)

    for t in range(2):
        wait_for(xb.at[0:3, t], in_send.at[t])
        wait_for((dk, dv)[t], own_recv.at[t])
        wait_for((dpk, dpv)[t], last_recv.at[t])
    wait_for(dqb.at[0:3], dq_send.at[0])
    wait_for(dq, dq_recv.at[0])
    wait_for(own_out.at[:, :, 0 : BLOCK - ROWS], kv_send.at[0])
    wait_for(own_out.at[:, :, 0 : BLOCK - ROWS], own_send.at[0])
    @pl.when(first_core)
    def _():
        wait_for(pre_out, fix_send.at[0])

    wait_for(pre_out.at[0, :, 0 : PREFIX - PIECE], last_send.at[0])
    wait_for(pre_in.at[0 : BLOCKS - 1], pre_send.at[0])
    for u in range(SLOTS):
        for at, sent in enumerate((5, 6, 3, 2)):

            @pl.when(place == at)
            def _():
                wait_for(kv.at[u, :, 0 : sent * BLOCK, :], win_send.at[u])

        for t in range(2):
            wait_for(part_out.at[u, t], part_send.at[u, t])


def hand_over(*refs):
    count = (len(refs) - 2) // 3
    before, after, held = refs[:count], refs[count : 2 * count], refs[2 * count : 3 * count]
    arrived, stored = refs[-2:]
    pieces = []
    for i in range(count):
        rows = before[i].shape[0]
        size = 16 if before[i].shape[1] > GROUP else rows
        for first in range(0, rows, size):
            n = len(pieces)
            part = pl.ds(first, size)
            pieces.append(
                (
                    pltpu.make_async_copy(before[i].at[part], held[i].at[part], arrived.at[n]),
                    pltpu.make_async_copy(held[i].at[part], after[i].at[part], stored.at[n]),
                )
            )
    for load, store in pieces:
        load.start()
    for load, store in pieces:
        load.wait()
        store.start()
    for load, store in pieces:
        store.wait()


def on_device(queries, keys, values, out_grad, prefix_keys, prefix_values, seg_ids, prefix_lens):
    bf16, f32 = jnp.bfloat16, jnp.float32
    dma = pltpu.SemaphoreType.DMA
    hbm = pl.BlockSpec(memory_space=pl.ANY)
    arrays = [
        ((STEPS, 2, BLOCK, WIDE), bf16),
        ((SLOTS, 2, KEYS, HEAD_DIM), bf16),
        ((KEYS, 128), bf16),
        ((BLOCK, 128), bf16),
        ((HEAD_DIM, KEYS), bf16),
        ((2, KEYS, HEAD_DIM), f32),
        ((SLOTS, 2, BLOCK, HEAD_DIM), f32),
        ((SPAN, WIDE), f32),
        ((SPAN, WIDE), f32),
        ((SPAN, WIDE), bf16),
        ((SPAN, GROUP), bf16),
        ((SPAN, WIDE), f32),
        ((SPAN, WIDE), f32),
        ((SPAN, WIDE), bf16),
        ((SPAN, GROUP), bf16),
        ((STEPS, BLOCK, WIDE), bf16),
        ((SLOTS, 2, BACK, BLOCK, HEAD_DIM), bf16),
        ((SLOTS, 2, BACK, BLOCK, HEAD_DIM), bf16),
        ((SLOTS, 2, 2, BLOCK, HEAD_DIM), bf16),
        ((SLOTS, 2, BLOCK, HEAD_DIM), bf16),
        ((SLOTS, 2, PREFIX, HEAD_DIM), bf16),
        ((BLOCKS, 2, PIECE, HEAD_DIM), bf16),
        ((2, PIECE, HEAD_DIM), bf16),
    ]
    semaphores = [
        2,
        1,
        SLOTS,
        1,
        1,
        1,
        SLOTS,
        (SLOTS, 2),
        2,
        STEPS,
        1,
        1,
        (SLOTS, 2),
        (SLOTS, 2),
        (SLOTS, 2),
        1,
        2,
        1,
        1,
        1,
        2,
    ]
    results = (
        jax.ShapeDtypeStruct(queries.shape, bf16),
        jax.ShapeDtypeStruct(keys.shape, bf16),
        jax.ShapeDtypeStruct(values.shape, bf16),
        jax.ShapeDtypeStruct(prefix_keys.shape, bf16),
        jax.ShapeDtypeStruct(prefix_values.shape, bf16),
    )
    raw = pl.pallas_call(
        kernel,
        out_shape=results,
        in_specs=[hbm] * 8,
        out_specs=(hbm,) * 5,
        scratch_shapes=[pltpu.VMEM(shape, kind) for shape, kind in arrays]
        + [pltpu.VMEM((64, 128), jnp.int32), pltpu.SMEM((SEGS,), jnp.int32)]
        + [dma(size if isinstance(size, tuple) else (size,)) for size in semaphores],
        compiler_params=pltpu.CompilerParams(
            collective_id=0, has_side_effects=True, vmem_limit_bytes=56 * 1024 * 1024
        ),
        cost_estimate=pl.CostEstimate(
            flops=4096 * SPAN * HEAD_DIM * 10,
            bytes_accessed=4 * 1024 * 1024,
            transcendentals=4096 * SPAN,
        ),
    )(
        queries,
        out_grad,
        keys,
        values,
        prefix_keys,
        prefix_values,
        seg_ids.reshape(64, 128),
        prefix_lens,
    )
    return pl.pallas_call(
        hand_over,
        out_shape=results,
        in_specs=[hbm] * len(results),
        out_specs=(hbm,) * len(results),
        scratch_shapes=[pltpu.VMEM(x.shape, x.dtype) for x in results] + [dma((16,)), dma((16,))],
    )(*raw)


def solution(mesh):
    return jax.shard_map(
        on_device,
        mesh=mesh,
        in_specs=(
            P(("seq", "head"), None),
            P(("seq", "head"), None),
            P(("seq", "head"), None),
            P(("seq", "head"), None),
            P(None, "head"),
            P(None, "head"),
            P(),
            P(),
        ),
        out_specs=(
            P(("seq", "head"), None),
            P(("seq", "head"), None),
            P(("seq", "head"), None),
            P(None, "head"),
            P(None, "head"),
        ),
        check_vma=False,
    )
```
